128 devices in a mesh: row: 8 (over z, core), col: 16 (over y, x).
Axes of the slice: x: 4, y: 4, z: 4, core: 2. Of those that a mesh axis runs over, the one named last changes fastest.
Arguments:
- integrals: bfloat16 [4096, 128, 2048], P('col', 'row'), may hold values from -6 to 6
- occupancy: int32 [32, 16], replicated, may hold values from 0 to 1
- coeffs: bfloat16 [2048, 256], replicated, may hold values from -0.125 to 0.125
- metric: bfloat16 [4096, 4096], P('col'), as said below
Outputs:
- fitted: bfloat16 [4096, 128, 256], P('col', 'row')
- pair_matrix: float32 [256, 256], replicated
The draws below stay inside these ranges and needn't reach their ends.
Inputs may be any that keep to these rules, and one draw needn't show every extreme that they name: metric is symmetric.
All inputs are finite; a program needn't handle non-finite values.
Results may differ from the reference program's by a relative error of at most 0.0037.
The reference program's roundings to bfloat16 on the way (of `masked` and `half`) count: a program that leaves them out, or rounds other values in their place, can miss the bound.
Values may be sent and summed in bfloat16 or wider, within the bound.
A program may use at most 192 MiB of HBM per device.

```python
import jax
import jax.numpy as jnp
from jax import lax

BLK = 128
NO = 256
NBB = 16
NP = 4096
NPB = 32
MU = 128
NB = 2048


def draw_occupancy(key, part):
    key = jax.random.fold_in(key, 1)
    first, second = jax.random.split(key)
    levels = jax.random.randint(first, (NPB, 1), 1, 9)
    rolls = jax.random.randint(second, (NPB, NBB), 0, 8)
    return (rolls < levels).astype(jnp.int32)


def draw_metric(key, part):
    key = jax.random.fold_in(key, 2)
    raw = jax.random.normal(key, (NP, NP), jnp.float32)
    scale = 0.5 / jnp.sqrt(jnp.float32(NP))
    sym = (raw + raw.T) * scale + 2.0 * jnp.eye(NP, dtype=jnp.float32)
    return sym.astype(jnp.bfloat16)


def block_levels(own_key, dims, pieces, low, largest):
    factor_of, own = 1.0, jax.random.fold_in(own_key, 6)
    for dim, blocks in pieces:
        heights = jnp.exp(jax.random.uniform(jax.random.fold_in(own, dim), (blocks,), jnp.float32, low / len(pieces), largest / len(pieces)))
        factor_of = factor_of * jnp.repeat(heights, dims[dim] // blocks).reshape([-1 if axis == dim else 1 for axis in range(len(dims))])
    return factor_of


def centred(stream_key, extent, spread, most, cuts=(), kind=jnp.bfloat16):
    entries = jax.random.normal(stream_key, extent, jnp.float32) * spread
    if len(cuts) > 0:
        entries = block_levels(stream_key, extent, cuts, -0.22, 0.18) * entries
    return jnp.clip(entries, min=-most, max=most).astype(kind)


def setup_inputs(seed: int = 0) -> dict:
    arg_keys = jax.random.split(jax.random.key(seed), 5)
    return {
        "integrals": centred(arg_keys[0], (NP, MU, NB), 1.0, 6.0, ((0, 16), (1, 8))),
        "occupancy": draw_occupancy(jax.random.fold_in(arg_keys[4], 71), 0),
        "coeffs": centred(arg_keys[2], (NB, NO), NB ** -0.5, 0.125),
        "metric": draw_metric(jax.random.fold_in(arg_keys[4], 71), 0),
    }


def reference(integrals, occupancy, coeffs, metric):
    blocks = integrals.reshape(NPB, BLK, MU, NBB, BLK)
    mask = occupancy.astype(integrals.dtype)
    masked = blocks * mask[:, None, None, :, None]
    half = jnp.dot(masked.reshape(NP * MU, NB), coeffs, preferred_element_type=jnp.float32).astype(jnp.bfloat16)
    half = half.reshape(NP, MU * NO)
    fitted = jnp.dot(metric, half, preferred_element_type=jnp.float32).astype(jnp.bfloat16)
    flat = fitted.reshape(NP * MU, NO)
    pairs = lax.dot_general(flat, flat, (((0,), (0,)), ((), ())), preferred_element_type=jnp.float32)
    pair_matrix = pairs / jnp.float32(NP * MU)
    return fitted.reshape(NP, MU, NO), pair_matrix
```

```python
import functools

import jax
import jax.numpy as jnp
from jax import lax
from jax.experimental import pallas as pl
from jax.experimental.pallas import tpu as pltpu
from jax.sharding import PartitionSpec as P

BLK = 128
NX = 4
NY = 4
QC = 32
UNIT = 2
AHEAD = 2
LAG = 1
NBUF = 4
OPP, RIGHT, LEFT, OWN = range(4)
MESH = pl.DeviceIdType.MESH
F32 = jnp.float32
BF16 = jnp.bfloat16


def kernel(
    dims, integrals, occupancy, coeffs, metric, fitted, pair,
    ibuf, cbuf, cmask, stage_a, stage_b, mb, mbt, hbuf, opp_out, side_out, opp_in, side_in,
    rows_f32, out_bf16, pbuf, pair_acc, red0, mine, red1, red2, red3, red4,
    in_sem, c_sem, m_loc, m_send, m_recv, m2_send, m2_recv, m3_send, m3_recv,
    ag_send, ag_recv, fw_send, fw_recv, op_send, op_recv, sd_send, sd_recv,
    r0_send, r0_recv, r1_send, r1_recv, r2_send, r2_recv, r3_send, r3_recv,
    r4_send, r4_recv, out_sem,
):
    ncol, nrow, rows, nmu, basis, no, scale = dims
    half = rows // 2
    kq = NX * rows
    per_set = nmu // 2
    nset = per_set // UNIT
    nz = nrow // 2
    row = lax.axis_index("row")
    sib = row + 1 - 2 * lax.rem(row, 2)
    col = lax.axis_index("col")
    x = lax.rem(col, NX)
    y = lax.div(col, NX)
    nab = rows // BLK
    nch = rows // QC

    def col_x(d):
        return y * NX + lax.rem(x + d, NX)

    def col_y(d):
        return lax.rem(y + d, NY) * NX + x

    ag_to = ((col_x(1), col_x(NX - 1)), (col_y(1), col_y(NY - 1)))
    rs_to = (ag_to[1], ag_to[0])
    at_x = tuple(lax.rem(x + d, NX) for d in (0, NX - 1, 1, 2))
    held = (at_x, (OWN, LEFT, RIGHT, OPP))

    def in_copy(ch):
        q = pl.ds(ch * QC, QC)
        slot = lax.rem(ch, NBUF)
        return pltpu.make_async_copy(integrals.at[q], ibuf.at[slot], in_sem.at[slot])

    c_copy = pltpu.make_async_copy(coeffs, cbuf, c_sem)
    c_copy.start()

    @pl.loop(0, NBUF)
    def _(ch):
        in_copy(ch).start()

    def m_own():
        src = metric.at[:, pl.ds(pl.multiple_of(y * kq, 128), kq)]
        return pltpu.make_async_copy(src, mb.at[OWN], m_loc)

    m_own().start()

    barrier = pltpu.get_barrier_semaphore()

    @pl.loop(1, ncol)
    def _(d):
        pl.semaphore_signal(
            barrier, inc=1, device_id=(row, lax.rem(col + d, ncol)), device_id_type=MESH
        )

    @pl.loop(1, nrow)
    def _(d):
        pl.semaphore_signal(
            barrier, inc=1, device_id=(lax.rem(row + d, nrow), col), device_id_type=MESH
        )

    slot_of = {1: RIGHT, 2: OPP, 3: LEFT}
    share = rows // nrow

    def rows_of(r):
        return pl.ds(pl.multiple_of(r * share, 16), share)

    def m_copy(d):
        yd = lax.rem(y + d, NY)
        return pltpu.make_async_remote_copy(
            src_ref=metric.at[rows_of(row), pl.ds(pl.multiple_of(yd * kq, 128), kq)],
            dst_ref=mb.at[slot_of[NY - d], rows_of(row)],
            send_sem=m_send.at[d - 1],
            recv_sem=m_recv.at[NY - d - 1],
            device_id=(row, col_y(d)),
            device_id_type=MESH,
        )

    def m_landed(s):
        return pltpu.make_async_remote_copy(
            src_ref=metric.at[rows_of(row), pl.ds(0, kq)],
            dst_ref=mb.at[slot_of[s], rows_of(row)],
            send_sem=m_send.at[s - 1],
            recv_sem=m_recv.at[s - 1],
            device_id=(row, col_y(s)),
            device_id_type=MESH,
        )

    def along_z(d):
        return lax.rem(row + 2 * d, nrow)

    def m_share(s, d):
        blk = mb.at[slot_of[s], rows_of(row)]
        return pltpu.make_async_remote_copy(
            src_ref=blk,
            dst_ref=blk,
            send_sem=m2_send.at[s - 1, d - 1],
            recv_sem=m2_recv.at[s - 1, nz - d - 1],
            device_id=(along_z(d), col),
            device_id_type=MESH,
        )

    def m_shared(s, d):
        blk = mb.at[slot_of[s], rows_of(along_z(d))]
        return pltpu.make_async_remote_copy(
            src_ref=blk,
            dst_ref=blk,
            send_sem=m2_send.at[s - 1, d - 1],
            recv_sem=m2_recv.at[s - 1, d - 1],
            device_id=(along_z(d), col),
            device_id_type=MESH,
        )

    def m_pass(s, d, mine=True):
        src = along_z(d) if mine else lax.rem(sib + 2 * d, nrow)
        blk = mb.at[slot_of[s], rows_of(src)]
        return pltpu.make_async_remote_copy(
            src_ref=blk,
            dst_ref=blk,
            send_sem=m3_send.at[s - 1, d],
            recv_sem=m3_recv.at[s - 1, d],
            device_id=(sib, col),
            device_id_type=MESH,
        )

    c_copy.wait()
    for ab in range(nab):

        @pl.loop(0, basis // BLK, unroll=4)
        def _(nb):
            on = jnp.full((BLK, no), occupancy[nb, col * nab + ab], jnp.int32) > 0
            at = pl.ds(pl.multiple_of(nb * BLK, BLK), BLK)
            kept = jnp.where(on, cbuf[at, :].astype(F32), 0.0)
            cmask[ab, at, :] = kept.astype(BF16)

    pl.semaphore_wait(barrier, ncol + nrow - 2)

    for d in (2, 1, 3):
        m_copy(d).start()

    def transform(ch, ab, to):
        rowsin = ibuf[lax.rem(ch, NBUF)].reshape(QC * nmu, basis)
        res = jnp.dot(rowsin, cmask[ab], preferred_element_type=F32)
        for h in range(no // 128):
            to[h] = res[:, h * 128 : (h + 1) * 128]

    def relayout(ch, frm):
        q0 = pl.multiple_of(ch * QC, QC)
        for mu in range(nmu):
            own = held[mu // per_set][0]
            for h in range(no // 128):
                got = frm[h, pl.ds(mu, QC, stride=nmu), :]
                hbuf[mu, own, pl.ds(q0, QC), h * 128 : (h + 1) * 128] = got.astype(BF16)

    def mus(st, k):
        return pl.ds(st * per_set + k * UNIT, UNIT)

    def ag_copy(st, side, k, hf, blk=None, to=None):
        part_rows = pl.ds(hf * half, half)
        src = held[st][0] if blk is None else blk
        dst = (at_x[0], (LEFT, RIGHT)[side])[st] if to is None else to
        return pltpu.make_async_remote_copy(
            src_ref=hbuf.at[mus(st, k), src, part_rows],
            dst_ref=hbuf.at[mus(st, k), dst, part_rows],
            send_sem=ag_send.at[st, side, k, hf],
            recv_sem=ag_recv.at[st, side, k, hf],
            device_id=(row, ag_to[st][side]),
            device_id_type=MESH,
        )

    def ag_wait(st, side, k, hf):
        blk = held[st][1 + side]
        ag_copy(st, side, k, hf, blk, blk).wait_recv()

    def fw_copy(st, side, k, blk=None, to=None):
        part_rows = pl.ds(side * half, half)
        src = held[st][1 + side] if blk is None else blk
        dst = (at_x[1 + side], OPP)[st] if to is None else to
        return pltpu.make_async_remote_copy(
            src_ref=hbuf.at[mus(st, k), src, part_rows],
            dst_ref=hbuf.at[mus(st, k), dst, part_rows],
            send_sem=fw_send.at[st, side, k],
            recv_sem=fw_recv.at[st, side, k],
            device_id=(row, ag_to[st][side]),
            device_id_type=MESH,
        )

    def fw_wait(st, side, k):
        blk = held[st][3]
        fw_copy(st, side, k, blk, blk).wait_recv()

    def op_copy(st, side, k):
        part_rows = pl.ds(side * half, half)
        return pltpu.make_async_remote_copy(
            src_ref=opp_out.at[mus(st, k), part_rows],
            dst_ref=opp_in.at[mus(st, k), part_rows],
            send_sem=op_send.at[st, side, k],
            recv_sem=op_recv.at[st, side, k],
            device_id=(row, rs_to[st][side]),
            device_id_type=MESH,
        )

    def sd_copy(st, side, mu):
        return pltpu.make_async_remote_copy(
            src_ref=side_out.at[side, mu],
            dst_ref=side_in.at[side, mu],
            send_sem=sd_send.at[side, mu],
            recv_sem=sd_recv.at[side, mu],
            device_id=(row, rs_to[st][side]),
            device_id_type=MESH,
        )

    def ag_start(st, k):
        for step in range(2):
            ag_copy(st, 0, k, step).start()
            ag_copy(st, 1, k, 1 - step).start()

    def forward(st, k):
        for side in range(2):
            ag_wait(st, side, k, side)
            fw_copy(st, side, k).start()

    def product(st, k):
        block = (mb, mbt)[st]
        for side in range(2):
            ag_wait(st, side, k, 1 - side)
            fw_wait(st, side, k)

        @pl.loop(0, UNIT)
        def _(m):
            mu = st * per_set + k * UNIT + m
            full = hbuf[mu].reshape(kq, no)
            got = jnp.dot(block[...].reshape(NY * rows, kq), full, preferred_element_type=F32)
            opp_out[mu] = got[:rows].astype(BF16)
            for side in range(2):
                at = (1 + side) * rows
                first = got[at : at + half]
                second = got[at + half : at + rows]
                plain = pl.ds((1 - side) * half, half)
                side_out[side, mu, plain] = (second, first)[side].astype(BF16)
                pbuf[st, lax.rem(k, 3), m, pl.ds(side * half, half)] = (first, second)[side]
            pbuf[st, lax.rem(k, 3), m, pl.ds(rows, rows)] = got[3 * rows :]

        op_copy(st, 0, k).start()
        op_copy(st, 1, k).start()

    def sides(k):
        for m in range(UNIT):
            for st in range(2):
                mu = st * per_set + k * UNIT + m
                for side in range(2):
                    if m == 0:
                        op_copy(st, side, k).wait_recv()
                    at = pl.ds(side * half, half)
                    side_out[side, mu, at] = (
                        pbuf[st, lax.rem(k, 3), m, at] + opp_in[mu, at].astype(F32)
                    ).astype(BF16)
                    sd_copy(st, side, mu).start()

    pair_acc[...] = jnp.zeros_like(pair_acc)

    def finish(k):
        @pl.loop(0, UNIT)
        def _(m):
            pairs = []
            for st in range(2):
                for side in range(2):
                    sd_copy(st, side, st * per_set + k * UNIT + m).wait_recv()
            for st in range(2):
                mu = st * per_set + k * UNIT + m
                own = pbuf[st, lax.rem(k, 3), m, pl.ds(rows, rows)]
                total = own + side_in[0, mu].astype(F32) + side_in[1, mu].astype(F32)
                done = total.astype(BF16)
                back = done.astype(F32)
                for h in range(no // 128):
                    at = pl.ds(mu, rows, stride=nmu)
                    rows_f32[h, at, :] = back[:, h * 128 : (h + 1) * 128]
                pairs.append(done)
            both = jnp.concatenate(pairs, axis=0)
            pair_acc[...] += lax.dot_general(
                both, both, (((0,), (0,)), ((), ())), preferred_element_type=F32
            )

    quarter = rows // 4

    def send_quarter(qt):
        part_rows = pl.ds(pl.multiple_of(qt * quarter, quarter), quarter)
        for k in range(AHEAD):
            for st in range(2):
                for side in range(2):
                    pltpu.make_async_remote_copy(
                        src_ref=hbuf.at[mus(st, k), held[st][0], part_rows],
                        dst_ref=hbuf.at[
                            mus(st, k), (at_x[0], (LEFT, RIGHT)[side])[st], part_rows
                        ],
                        send_sem=ag_send.at[st, side, k, lax.div(qt, 2)],
                        recv_sem=ag_recv.at[st, side, k, lax.div(qt, 2)],
                        device_id=(row, ag_to[st][side]),
                        device_id_type=MESH,
                    ).start()

    stage_b[...] = jnp.zeros_like(stage_b)

    @pl.loop(0, nch // 2)
    def _(j):
        ch = 2 * j
        ab = lax.div(ch * QC, BLK)
        in_copy(ch).wait()
        in_copy(ch + 1).wait()
        transform(ch, ab, stage_a)
        relayout(lax.max(ch - 1, 0), stage_b)

        @pl.when(j >= 1)
        def _():
            send_quarter(j - 1)

        @pl.when(j == 1)
        def _():
            for s in (2, 1, 3):
                m_landed(s).wait_recv()
                for d in (2, 1, 3):
                    m_share(s, d).start()
                m_pass(s, 0).start()

        transform(ch + 1, ab, stage_b)
        relayout(ch, stage_a)

        @pl.when(ch + NBUF < nch)
        def _():
            in_copy(ch + NBUF).start()
            in_copy(ch + NBUF + 1).start()

    relayout(nch - 1, stage_b)
    send_quarter(nch // 2 - 1)

    def metric_sent():
        for s in range(1, NY):
            m_copy(s).wait_send()
            for d in range(nz):
                m_pass(s, d).wait_send()
            for d in range(1, nz):
                m_share(s, d).wait_send()

    def sent_early(k):
        for st in range(2):
            for side in range(2):
                for hf in range(2):
                    ag_copy(st, side, k, hf).wait_send()
                fw_copy(st, side, k).wait_send()
                op_copy(st, side, k).wait_send()

    def sent_late(k):
        for st in range(2):
            for side in range(2):
                for m in range(UNIT):
                    sd_copy(st, side, st * per_set + k * UNIT + m).wait_send()

    def metric_ready():
        m_own().wait()
        for d in range(nz):
            for s in (2, 1, 3):
                m_pass(s, d, False).wait_recv()

    def transpose_metric():
        offs = {OPP: 2, RIGHT: 1, LEFT: NX - 1, OWN: 0}
        for to, d in offs.items():
            at = pl.ds(pl.multiple_of(lax.rem(x + d, NX) * rows, 128), rows)

            @pl.loop(0, NY)
            def _(s):
                mbt[to, :, pl.ds(pl.multiple_of(s * rows, 128), rows)] = mb[s, :, at].T

    @pl.loop(0, nset + LAG + 2)
    def _(k):
        @pl.when(k + AHEAD < nset)
        def _():
            ag_start(0, k + AHEAD)
            ag_start(1, k + AHEAD)

        @pl.when(k < nset)
        def _():
            forward(0, k)
            forward(1, k)

        @pl.when(k == 0)
        def _():
            for s in (2, 1, 3):
                for d in (1, 3, 2):
                    m_shared(s, d).wait_recv()
                    m_pass(s, d).start()

        @pl.when((k >= LAG) & (k < nset + LAG))
        def _():
            @pl.when(k == LAG)
            def _():
                metric_ready()

            product(0, k - LAG)

            @pl.when(k == LAG)
            def _():
                transpose_metric()

            product(1, k - LAG)

        @pl.when((k >= LAG + 1) & (k < nset + LAG + 1))
        def _():
            sides(k - LAG - 1)
            sent_early(k - LAG - 1)

        @pl.when(k == LAG + 1)
        def _():
            metric_sent()

        @pl.when(k >= LAG + 2)
        def _():
            finish(k - LAG - 2)

        @pl.when((k >= LAG + 2) & (k < nset + LAG + 1))
        def _():
            sent_late(k - LAG - 2)

    chunk = no // 2 // ncol
    core = lax.rem(row, 2)
    mid = no // 2
    mine_at = pl.ds(pl.multiple_of(core * mid, 8), mid)
    theirs_at = pl.ds(pl.multiple_of((1 - core) * mid, 8), mid)

    r0_copy = pltpu.make_async_remote_copy(
        src_ref=pair_acc.at[theirs_at],
        dst_ref=red0,
        send_sem=r0_send,
        recv_sem=r0_recv,
        device_id=(sib, col),
        device_id_type=MESH,
    )
    r0_copy.start()

    def r1_copy(d):
        to = lax.rem(col + d, ncol)
        return pltpu.make_async_remote_copy(
            src_ref=mine.at[to],
            dst_ref=red1.at[col],
            send_sem=r1_send.at[d],
            recv_sem=r1_recv.at[col],
            device_id=(row, to),
            device_id_type=MESH,
        )

    def r1_landed(src):
        return pltpu.make_async_remote_copy(
            src_ref=mine.at[src],
            dst_ref=red1.at[src],
            send_sem=r1_send.at[0],
            recv_sem=r1_recv.at[src],
            device_id=(row, src),
            device_id_type=MESH,
        )

    def r2_copy(d):
        z = lax.div(row, 2)
        return pltpu.make_async_remote_copy(
            src_ref=red2.at[z],
            dst_ref=red2.at[z],
            send_sem=r2_send.at[d],
            recv_sem=r2_recv.at[z],
            device_id=(along_z(d), col),
            device_id_type=MESH,
        )

    def r2_landed(d):
        z = lax.div(along_z(d), 2)
        return pltpu.make_async_remote_copy(
            src_ref=red2.at[z],
            dst_ref=red2.at[z],
            send_sem=r2_send.at[d],
            recv_sem=r2_recv.at[z],
            device_id=(along_z(d), col),
            device_id_type=MESH,
        )

    def r3_copy(d):
        to = lax.rem(col + d, ncol)
        return pltpu.make_async_remote_copy(
            src_ref=red3.at[col],
            dst_ref=red3.at[col],
            send_sem=r3_send.at[d],
            recv_sem=r3_recv.at[col],
            device_id=(row, to),
            device_id_type=MESH,
        )

    def r3_landed(src):
        return pltpu.make_async_remote_copy(
            src_ref=red3.at[src],
            dst_ref=red3.at[src],
            send_sem=r3_send.at[0],
            recv_sem=r3_recv.at[src],
            device_id=(row, src),
            device_id_type=MESH,
        )

    def lay_out(begin, end):
        @pl.loop(begin, end)
        def _(ch):
            at = pl.ds(pl.multiple_of(ch * QC * nmu, QC), QC * nmu)
            for h in range(no // 128):
                out_bf16[pl.ds(ch * QC, QC), :, h * 128 : (h + 1) * 128] = (
                    rows_f32[h, at, :].astype(BF16).reshape(QC, nmu, 128)
                )

    lay_out(0, nch // 4)
    r0_copy.wait_recv()
    mine[...] = (pair_acc[mine_at] + red0[...]).reshape(ncol, chunk, no)

    @pl.loop(1, ncol, unroll=5)
    def _(d):
        r1_copy(d).start()

    red1[col] = mine[col]

    lay_out(nch // 4, nch)
    sent_late(nset - 1)

    out_copy = pltpu.make_async_copy(out_bf16, fitted, out_sem)
    out_copy.start()

    @pl.loop(1, ncol)
    def _(d):
        r1_landed(lax.rem(col + d, ncol)).wait_recv()

    total = red1[0]
    for c in range(1, ncol):
        total = total + red1[c]
    red2[lax.div(row, 2)] = total
    for d in (2, 1, 3):
        r2_copy(d).start()
    for d in (1, 3, 2):
        r2_landed(d).wait_recv()

    total = red2[0]
    for z in range(1, nz):
        total = total + red2[z]
    red3[col] = total * F32(scale)

    @pl.loop(1, ncol, unroll=5)
    def _(d):
        r3_copy(d).start()

    @pl.loop(1, ncol, unroll=5)
    def _(d):
        r3_landed(lax.rem(col + d, ncol)).wait_recv()

    r4_copy = pltpu.make_async_remote_copy(
        src_ref=red3,
        dst_ref=red4,
        send_sem=r4_send,
        recv_sem=r4_recv,
        device_id=(sib, col),
        device_id_type=MESH,
    )
    r4_copy.start()
    pair[mine_at] = red3[...].reshape(mid, no)

    r0_copy.wait_send()

    @pl.loop(1, ncol)
    def _(d):
        r1_copy(d).wait_send()
        r3_copy(d).wait_send()

    for d in range(1, nz):
        r2_copy(d).wait_send()

    r4_copy.wait_recv()
    pair[theirs_at] = red4[...].reshape(mid, no)
    r4_copy.wait_send()
    out_copy.wait()


def on_device(ncol, nrow, integrals, occupancy, coeffs, metric):
    rows, nmu, basis = integrals.shape
    no = coeffs.shape[1]
    kq = NX * rows
    chunk = no // 2 // ncol
    scale = 1.0 / (rows * ncol * nmu * nrow)
    dims = (ncol, nrow, rows, nmu, basis, no, scale)
    lanes = no // 128
    dma = pltpu.SemaphoreType.DMA
    scratch = [
        pltpu.VMEM((NBUF, QC, nmu, basis), BF16),
        pltpu.VMEM((basis, no), BF16),
        pltpu.VMEM((rows // BLK, basis, no), BF16),
        pltpu.VMEM((lanes, QC * nmu, 128), F32),
        pltpu.VMEM((lanes, QC * nmu, 128), F32),
        pltpu.VMEM((NY, rows, kq), BF16),
        pltpu.VMEM((NX, rows, kq), BF16),
        pltpu.VMEM((nmu, NX, rows, no), BF16),
        pltpu.VMEM((nmu, rows, no), BF16),
        pltpu.VMEM((2, nmu, rows, no), BF16),
        pltpu.VMEM((nmu, rows, no), BF16),
        pltpu.VMEM((2, nmu, rows, no), BF16),
        pltpu.VMEM((lanes, rows * nmu, 128), F32),
        pltpu.VMEM((rows, nmu, no), BF16),
        pltpu.VMEM((2, 3, UNIT, 2 * rows, no), F32),
        pltpu.VMEM((no, no), F32),
        pltpu.VMEM((no // 2, no), F32),
        pltpu.VMEM((ncol, chunk, no), F32),
        pltpu.VMEM((ncol, chunk, no), F32),
        pltpu.VMEM((nrow // 2, chunk, no), F32),
        pltpu.VMEM((ncol, chunk, no), F32),
        pltpu.VMEM((ncol, chunk, no), F32),
        dma((NBUF,)),
        dma,
        dma,
        dma((NY - 1,)),
        dma((NY - 1,)),
        dma((NY - 1, nrow // 2 - 1)),
        dma((NY - 1, nrow // 2 - 1)),
        dma((NY - 1, nrow // 2)),
        dma((NY - 1, nrow // 2)),
        dma((2, 2, nmu // 2 // UNIT, 2)),
        dma((2, 2, nmu // 2 // UNIT, 2)),
        dma((2, 2, nmu // 2 // UNIT)),
        dma((2, 2, nmu // 2 // UNIT)),
        dma((2, 2, nmu // 2 // UNIT)),
        dma((2, 2, nmu // 2 // UNIT)),
        dma((2, nmu)),
        dma((2, nmu)),
        dma,
        dma,
        dma((ncol,)),
        dma((ncol,)),
        dma((nrow // 2,)),
        dma((nrow // 2,)),
        dma((ncol,)),
        dma((ncol,)),
        dma,
        dma,
        dma,
    ]
    anywhere = pl.BlockSpec(memory_space=pl.ANY)
    flops = 2 * rows * nmu * no * (basis + ncol * rows + no)
    return pl.pallas_call(
        functools.partial(kernel, dims),
        out_shape=(
            pltpu.VMEM((rows, nmu, no), BF16),
            pltpu.VMEM((no, no), F32),
        ),
        in_specs=[
            anywhere,
            pl.BlockSpec(memory_space=pltpu.SMEM),
            anywhere,
            anywhere,
        ],
        out_specs=(anywhere, pl.BlockSpec(memory_space=pltpu.VMEM)),
        scratch_shapes=scratch,
        compiler_params=pltpu.CompilerParams(
            collective_id=0, has_side_effects=True, vmem_limit_bytes=58 * 1024 * 1024
        ),
        cost_estimate=pl.CostEstimate(
            flops=flops, bytes_accessed=2 * rows * nmu * (basis + no), transcendentals=0
        ),
    )(integrals, occupancy.T, coeffs, metric)


def solution(mesh):
    placed = (P("col", "row", None), P(), P(), P("col", None))
    return jax.shard_map(
        functools.partial(on_device, mesh.shape["col"], mesh.shape["row"]),
        mesh=mesh,
        in_specs=placed,
        out_specs=(P("col", "row", None), P()),
        check_vma=False,
    )
```

```python
import functools

import jax
import jax.numpy as jnp
from jax import lax
from jax.experimental import pallas as pl
from jax.experimental.pallas import tpu as pltpu
from jax.sharding import PartitionSpec as P

BLK = 128
NX = 4
NY = 4
QC = 32
UNIT = 2
AHEAD = 2
LAG = 1
NBUF = 4
OPP, RIGHT, LEFT, OWN = range(4)
MESH = pl.DeviceIdType.MESH
F32 = jnp.float32
BF16 = jnp.bfloat16


def kernel(
    dims, integrals, occupancy, coeffs, metric, fitted, pair,
    ibuf, cbuf, cmask, stage_a, stage_b, mb, mbt, hbuf, opp_out, side_out, opp_in, side_in,
    rows_f32, out_bf16, pbuf, pair_acc, red0, mine, red1, red2, red3, red4,
    in_sem, c_sem, m_loc, m_send, m_recv, m2_send, m2_recv, m3_send, m3_recv,
    ag_send, ag_recv, fw_send, fw_recv, op_send, op_recv, sd_send, sd_recv,
    r0_send, r0_recv, r1_send, r1_recv, r2_send, r2_recv, r3_send, r3_recv,
    r4_send, r4_recv, out_sem,
):
    ncol, nrow, rows, nmu, basis, no, scale = dims
    half = rows // 2
    kq = NX * rows
    per_set = nmu // 2
    nset = per_set // UNIT
    nz = nrow // 2
    row = lax.axis_index("row")
    sib = row + 1 - 2 * lax.rem(row, 2)
    col = lax.axis_index("col")
    x = lax.rem(col, NX)
    y = lax.div(col, NX)
    nab = rows // BLK
    nch = rows // QC

    def col_x(d):
        return y * NX + lax.rem(x + d, NX)

    def col_y(d):
        return lax.rem(y + d, NY) * NX + x

    ag_to = ((col_x(1), col_x(NX - 1)), (col_y(1), col_y(NY - 1)))
    rs_to = (ag_to[1], ag_to[0])
    at_x = tuple(lax.rem(x + d, NX) for d in (0, NX - 1, 1, 2))
    held = (at_x, (OWN, LEFT, RIGHT, OPP))

    def in_copy(ch):
        q = pl.ds(ch * QC, QC)
        slot = lax.rem(ch, NBUF)
        return pltpu.make_async_copy(integrals.at[q], ibuf.at[slot], in_sem.at[slot])

    c_copy = pltpu.make_async_copy(coeffs, cbuf, c_sem)
    c_copy.start()

    @pl.loop(0, NBUF)
    def _(ch):
        in_copy(ch).start()

    def m_own():
        src = metric.at[:, pl.ds(pl.multiple_of(y * kq, 128), kq)]
        return pltpu.make_async_copy(src, mb.at[OWN], m_loc)

    m_own().start()

    barrier = pltpu.get_barrier_semaphore()

    @pl.loop(1, ncol)
    def _(d):
        pl.semaphore_signal(
            barrier, inc=1, device_id=(row, lax.rem(col + d, ncol)), device_id_type=MESH
        )

    @pl.loop(1, nrow)
    def _(d):
        pl.semaphore_signal(
            barrier, inc=1, device_id=(lax.rem(row + d, nrow), col), device_id_type=MESH
        )

    slot_of = {1: RIGHT, 2: OPP, 3: LEFT}
    share = rows // nrow

    def rows_of(r):
        return pl.ds(pl.multiple_of(r * share, 16), share)

    def m_copy(d):
        yd = lax.rem(y + d, NY)
        return pltpu.make_async_remote_copy(
            src_ref=metric.at[rows_of(row), pl.ds(pl.multiple_of(yd * kq, 128), kq)],
            dst_ref=mb.at[slot_of[NY - d], rows_of(row)],
            send_sem=m_send.at[d - 1],
            recv_sem=m_recv.at[NY - d - 1],
            device_id=(row, col_y(d)),
            device_id_type=MESH,
        )

    def m_landed(s):
        return pltpu.make_async_remote_copy(
            src_ref=metric.at[rows_of(row), pl.ds(0, kq)],
            dst_ref=mb.at[slot_of[s], rows_of(row)],
            send_sem=m_send.at[s - 1],
            recv_sem=m_recv.at[s - 1],
            device_id=(row, col_y(s)),
            device_id_type=MESH,
        )

    def along_z(d):
        return lax.rem(row + 2 * d, nrow)

    def m_share(s, d):
        blk = mb.at[slot_of[s], rows_of(row)]
        return pltpu.make_async_remote_copy(
            src_ref=blk,
            dst_ref=blk,
            send_sem=m2_send.at[s - 1, d - 1],
            recv_sem=m2_recv.at[s - 1, nz - d - 1],
            device_id=(along_z(d), col),
            device_id_type=MESH,
        )

    def m_shared(s, d):
        blk = mb.at[slot_of[s], rows_of(along_z(d))]
        return pltpu.make_async_remote_copy(
            src_ref=blk,
            dst_ref=blk,
            send_sem=m2_send.at[s - 1, d - 1],
            recv_sem=m2_recv.at[s - 1, d - 1],
            device_id=(along_z(d), col),
            device_id_type=MESH,
        )

    def m_pass(s, d, mine=True):
        src = along_z(d) if mine else lax.rem(sib + 2 * d, nrow)
        blk = mb.at[slot_of[s], rows_of(src)]
        return pltpu.make_async_remote_copy(
            src_ref=blk,
            dst_ref=blk,
            send_sem=m3_send.at[s - 1, d],
            recv_sem=m3_recv.at[s - 1, d],
            device_id=(sib, col),
            device_id_type=MESH,
        )

    c_copy.wait()
    def make_mask(ab):
        @pl.loop(0, basis // BLK, unroll=4)
        def _(nb):
            on = jnp.full((BLK, no), occupancy[nb, col * nab + ab], jnp.int32) > 0
            at = pl.ds(pl.multiple_of(nb * BLK, BLK), BLK)
            kept = jnp.where(on, cbuf[at, :].astype(F32), 0.0)
            cmask[ab, at, :] = kept.astype(BF16)

    make_mask(0)

    pl.semaphore_wait(barrier, ncol + nrow - 2)

    for d in (2, 1, 3):
        m_copy(d).start()

    def transform(ch, ab, to):
        rowsin = ibuf[lax.rem(ch, NBUF)].reshape(QC * nmu, basis)
        res = jnp.dot(rowsin, cmask[ab], preferred_element_type=F32)
        for h in range(no // 128):
            to[h] = res[:, h * 128 : (h + 1) * 128]

    def relayout(ch, frm):
        q0 = pl.multiple_of(ch * QC, QC)
        for mu in range(nmu):
            own = held[mu // per_set][0]
            for h in range(no // 128):
                got = frm[h, pl.ds(mu, QC, stride=nmu), :]
                hbuf[mu, own, pl.ds(q0, QC), h * 128 : (h + 1) * 128] = got.astype(BF16)

    def mus(st, k):
        return pl.ds(st * per_set + k * UNIT, UNIT)

    def ag_copy(st, side, k, hf, blk=None, to=None):
        part_rows = pl.ds(hf * half, half)
        src = held[st][0] if blk is None else blk
        dst = (at_x[0], (LEFT, RIGHT)[side])[st] if to is None else to
        return pltpu.make_async_remote_copy(
            src_ref=hbuf.at[mus(st, k), src, part_rows],
            dst_ref=hbuf.at[mus(st, k), dst, part_rows],
            send_sem=ag_send.at[st, side, k, hf],
            recv_sem=ag_recv.at[st, side, k, hf],
            device_id=(row, ag_to[st][side]),
            device_id_type=MESH,
        )

    def ag_wait(st, side, k, hf):
        blk = held[st][1 + side]
        ag_copy(st, side, k, hf, blk, blk).wait_recv()

    def fw_copy(st, side, k, blk=None, to=None):
        part_rows = pl.ds(side * half, half)
        src = held[st][1 + side] if blk is None else blk
        dst = (at_x[1 + side], OPP)[st] if to is None else to
        return pltpu.make_async_remote_copy(
            src_ref=hbuf.at[mus(st, k), src, part_rows],
            dst_ref=hbuf.at[mus(st, k), dst, part_rows],
            send_sem=fw_send.at[st, side, k],
            recv_sem=fw_recv.at[st, side, k],
            device_id=(row, ag_to[st][side]),
            device_id_type=MESH,
        )

    def fw_wait(st, side, k):
        blk = held[st][3]
        fw_copy(st, side, k, blk, blk).wait_recv()

    def op_copy(st, side, k):
        part_rows = pl.ds(side * half, half)
        return pltpu.make_async_remote_copy(
            src_ref=opp_out.at[mus(st, k), part_rows],
            dst_ref=opp_in.at[mus(st, k), part_rows],
            send_sem=op_send.at[st, side, k],
            recv_sem=op_recv.at[st, side, k],
            device_id=(row, rs_to[st][side]),
            device_id_type=MESH,
        )

    def sd_copy(st, side, mu):
        return pltpu.make_async_remote_copy(
            src_ref=side_out.at[side, mu],
            dst_ref=side_in.at[side, mu],
            send_sem=sd_send.at[side, mu],
            recv_sem=sd_recv.at[side, mu],
            device_id=(row, rs_to[st][side]),
            device_id_type=MESH,
        )

    def ag_start(st, k):
        for step in range(2):
            ag_copy(st, 0, k, step).start()
            ag_copy(st, 1, k, 1 - step).start()

    def forward(st, k):
        for side in range(2):
            ag_wait(st, side, k, side)
            fw_copy(st, side, k).start()

    def product(st, k):
        block = (mb, mbt)[st]
        for side in range(2):
            ag_wait(st, side, k, 1 - side)
            fw_wait(st, side, k)

        @pl.loop(0, UNIT)
        def _(m):
            mu = st * per_set + k * UNIT + m
            full = hbuf[mu].reshape(kq, no)
            got = jnp.dot(block[...].reshape(NY * rows, kq), full, preferred_element_type=F32)
            opp_out[mu] = got[:rows].astype(BF16)
            for side in range(2):
                at = (1 + side) * rows
                first = got[at : at + half]
                second = got[at + half : at + rows]
                plain = pl.ds((1 - side) * half, half)
                side_out[side, mu, plain] = (second, first)[side].astype(BF16)
                pbuf[st, lax.rem(k, 3), m, pl.ds(side * half, half)] = (first, second)[side]
            pbuf[st, lax.rem(k, 3), m, pl.ds(rows, rows)] = got[3 * rows :]

        op_copy(st, 0, k).start()
        op_copy(st, 1, k).start()

    def sides(k):
        for m in range(UNIT):
            for st in range(2):
                mu = st * per_set + k * UNIT + m
                for side in range(2):
                    if m == 0:
                        op_copy(st, side, k).wait_recv()
                    at = pl.ds(side * half, half)
                    side_out[side, mu, at] = (
                        pbuf[st, lax.rem(k, 3), m, at] + opp_in[mu, at].astype(F32)
                    ).astype(BF16)
                    sd_copy(st, side, mu).start()

    pair_acc[...] = jnp.zeros_like(pair_acc)

    def finish(k):
        @pl.loop(0, UNIT)
        def _(m):
            pairs = []
            for st in range(2):
                for side in range(2):
                    sd_copy(st, side, st * per_set + k * UNIT + m).wait_recv()
            for st in range(2):
                mu = st * per_set + k * UNIT + m
                own = pbuf[st, lax.rem(k, 3), m, pl.ds(rows, rows)]
                total = own + side_in[0, mu].astype(F32) + side_in[1, mu].astype(F32)
                done = total.astype(BF16)
                back = done.astype(F32)
                for h in range(no // 128):
                    at = pl.ds(mu, rows, stride=nmu)
                    rows_f32[h, at, :] = back[:, h * 128 : (h + 1) * 128]
                pairs.append(done)
            both = jnp.concatenate(pairs, axis=0)
            pair_acc[...] += lax.dot_general(
                both, both, (((0,), (0,)), ((), ())), preferred_element_type=F32
            )

    quarter = rows // 4

    def send_quarter(qt):
        part_rows = pl.ds(pl.multiple_of(qt * quarter, quarter), quarter)
        for k in range(AHEAD):
            for st in range(2):
                for side in range(2):
                    pltpu.make_async_remote_copy(
                        src_ref=hbuf.at[mus(st, k), held[st][0], part_rows],
                        dst_ref=hbuf.at[
                            mus(st, k), (at_x[0], (LEFT, RIGHT)[side])[st], part_rows
                        ],
                        send_sem=ag_send.at[st, side, k, lax.div(qt, 2)],
                        recv_sem=ag_recv.at[st, side, k, lax.div(qt, 2)],
                        device_id=(row, ag_to[st][side]),
                        device_id_type=MESH,
                    ).start()

    stage_b[...] = jnp.zeros_like(stage_b)

    @pl.loop(0, nch // 2)
    def _(j):
        ch = 2 * j
        ab = lax.div(ch * QC, BLK)

        for later in range(1, nab):

            @pl.when(ch == later * (nch // nab))
            def _():
                make_mask(later)

        in_copy(ch).wait()
        in_copy(ch + 1).wait()
        transform(ch, ab, stage_a)
        relayout(lax.max(ch - 1, 0), stage_b)

        @pl.when(j >= 1)
        def _():
            send_quarter(j - 1)

        @pl.when(j == 1)
        def _():
            for s in (2, 1, 3):
                m_landed(s).wait_recv()
                for d in (2, 1, 3):
                    m_share(s, d).start()
                m_pass(s, 0).start()

        transform(ch + 1, ab, stage_b)
        relayout(ch, stage_a)

        @pl.when(ch + NBUF < nch)
        def _():
            in_copy(ch + NBUF).start()
            in_copy(ch + NBUF + 1).start()

    relayout(nch - 1, stage_b)
    send_quarter(nch // 2 - 1)

    def metric_sent():
        for s in range(1, NY):
            m_copy(s).wait_send()
            for d in range(nz):
                m_pass(s, d).wait_send()
            for d in range(1, nz):
                m_share(s, d).wait_send()

    def sent_early(k):
        for st in range(2):
            for side in range(2):
                for hf in range(2):
                    ag_copy(st, side, k, hf).wait_send()
                fw_copy(st, side, k).wait_send()
                op_copy(st, side, k).wait_send()

    def sent_late(k):
        for st in range(2):
            for side in range(2):
                for m in range(UNIT):
                    sd_copy(st, side, st * per_set + k * UNIT + m).wait_send()

    def metric_ready():
        m_own().wait()
        for d in range(nz):
            for s in (2, 1, 3):
                m_pass(s, d, False).wait_recv()

    def transpose_metric():
        offs = {OPP: 2, RIGHT: 1, LEFT: NX - 1, OWN: 0}
        for to, d in offs.items():
            at = pl.ds(pl.multiple_of(lax.rem(x + d, NX) * rows, 128), rows)

            @pl.loop(0, NY)
            def _(s):
                mbt[to, :, pl.ds(pl.multiple_of(s * rows, 128), rows)] = mb[s, :, at].T

    @pl.loop(0, nset + LAG + 2)
    def _(k):
        @pl.when(k + AHEAD < nset)
        def _():
            ag_start(0, k + AHEAD)
            ag_start(1, k + AHEAD)

        @pl.when(k < nset)
        def _():
            forward(0, k)
            forward(1, k)

        @pl.when(k == 0)
        def _():
            for s in (2, 1, 3):
                for d in (1, 3, 2):
                    m_shared(s, d).wait_recv()
                    m_pass(s, d).start()

        @pl.when(k == nset + LAG - 1)
        def _():
            sides(k - LAG - 1)

        @pl.when((k >= LAG) & (k < nset + LAG))
        def _():
            @pl.when(k == LAG)
            def _():
                metric_ready()

            product(0, k - LAG)

            @pl.when(k == LAG)
            def _():
                transpose_metric()

            product(1, k - LAG)

        @pl.when((k >= LAG + 1) & (k < nset + LAG + 1) & (k != nset + LAG - 1))
        def _():
            sides(k - LAG - 1)

        @pl.when((k >= LAG + 1) & (k < nset + LAG + 1))
        def _():
            sent_early(k - LAG - 1)

        @pl.when(k == LAG + 1)
        def _():
            metric_sent()

        @pl.when(k >= LAG + 2)
        def _():
            finish(k - LAG - 2)

        @pl.when((k >= LAG + 2) & (k < nset + LAG + 1))
        def _():
            sent_late(k - LAG - 2)

    chunk = no // 2 // ncol
    core = lax.rem(row, 2)
    mid = no // 2
    mine_at = pl.ds(pl.multiple_of(core * mid, 8), mid)
    theirs_at = pl.ds(pl.multiple_of((1 - core) * mid, 8), mid)

    r0_copy = pltpu.make_async_remote_copy(
        src_ref=pair_acc.at[theirs_at],
        dst_ref=red0,
        send_sem=r0_send,
        recv_sem=r0_recv,
        device_id=(sib, col),
        device_id_type=MESH,
    )
    r0_copy.start()

    def r1_copy(d):
        to = lax.rem(col + d, ncol)
        return pltpu.make_async_remote_copy(
            src_ref=mine.at[to],
            dst_ref=red1.at[col],
            send_sem=r1_send.at[d],
            recv_sem=r1_recv.at[col],
            device_id=(row, to),
            device_id_type=MESH,
        )

    def r1_landed(src):
        return pltpu.make_async_remote_copy(
            src_ref=mine.at[src],
            dst_ref=red1.at[src],
            send_sem=r1_send.at[0],
            recv_sem=r1_recv.at[src],
            device_id=(row, src),
            device_id_type=MESH,
        )

    def r2_copy(d):
        z = lax.div(row, 2)
        return pltpu.make_async_remote_copy(
            src_ref=red2.at[z],
            dst_ref=red2.at[z],
            send_sem=r2_send.at[d],
            recv_sem=r2_recv.at[z],
            device_id=(along_z(d), col),
            device_id_type=MESH,
        )

    def r2_landed(d):
        z = lax.div(along_z(d), 2)
        return pltpu.make_async_remote_copy(
            src_ref=red2.at[z],
            dst_ref=red2.at[z],
            send_sem=r2_send.at[d],
            recv_sem=r2_recv.at[z],
            device_id=(along_z(d), col),
            device_id_type=MESH,
        )

    def r3_copy(d):
        to = lax.rem(col + d, ncol)
        return pltpu.make_async_remote_copy(
            src_ref=red3.at[col],
            dst_ref=red3.at[col],
            send_sem=r3_send.at[d],
            recv_sem=r3_recv.at[col],
            device_id=(row, to),
            device_id_type=MESH,
        )

    def r3_landed(src):
        return pltpu.make_async_remote_copy(
            src_ref=red3.at[src],
            dst_ref=red3.at[src],
            send_sem=r3_send.at[0],
            recv_sem=r3_recv.at[src],
            device_id=(row, src),
            device_id_type=MESH,
        )

    def lay_out(begin, end):
        @pl.loop(begin, end)
        def _(ch):
            at = pl.ds(pl.multiple_of(ch * QC * nmu, QC), QC * nmu)
            for h in range(no // 128):
                out_bf16[pl.ds(ch * QC, QC), :, h * 128 : (h + 1) * 128] = (
                    rows_f32[h, at, :].astype(BF16).reshape(QC, nmu, 128)
                )

    lay_out(0, nch // 4)
    r0_copy.wait_recv()
    mine[...] = (pair_acc[mine_at] + red0[...]).reshape(ncol, chunk, no)

    @pl.loop(1, ncol, unroll=5)
    def _(d):
        r1_copy(d).start()

    red1[col] = mine[col]

    lay_out(nch // 4, nch)
    sent_late(nset - 1)

    out_copy = pltpu.make_async_copy(out_bf16, fitted, out_sem)
    out_copy.start()

    @pl.loop(1, ncol)
    def _(d):
        r1_landed(lax.rem(col + d, ncol)).wait_recv()

    total = red1[0]
    for c in range(1, ncol):
        total = total + red1[c]
    red2[lax.div(row, 2)] = total
    for d in (2, 1, 3):
        r2_copy(d).start()
    for d in (1, 3, 2):
        r2_landed(d).wait_recv()

    total = red2[0]
    for z in range(1, nz):
        total = total + red2[z]
    red3[col] = total * F32(scale)

    @pl.loop(1, ncol, unroll=5)
    def _(d):
        r3_copy(d).start()

    @pl.loop(1, ncol, unroll=5)
    def _(d):
        r3_landed(lax.rem(col + d, ncol)).wait_recv()

    r4_copy = pltpu.make_async_remote_copy(
        src_ref=red3,
        dst_ref=red4,
        send_sem=r4_send,
        recv_sem=r4_recv,
        device_id=(sib, col),
        device_id_type=MESH,
    )
    r4_copy.start()
    pair[mine_at] = red3[...].reshape(mid, no)

    r0_copy.wait_send()

    @pl.loop(1, ncol)
    def _(d):
        r1_copy(d).wait_send()
        r3_copy(d).wait_send()

    for d in range(1, nz):
        r2_copy(d).wait_send()

    r4_copy.wait_recv()
    pair[theirs_at] = red4[...].reshape(mid, no)
    r4_copy.wait_send()
    out_copy.wait()


def on_device(ncol, nrow, integrals, occupancy, coeffs, metric):
    rows, nmu, basis = integrals.shape
    no = coeffs.shape[1]
    kq = NX * rows
    chunk = no // 2 // ncol
    scale = 1.0 / (rows * ncol * nmu * nrow)
    dims = (ncol, nrow, rows, nmu, basis, no, scale)
    lanes = no // 128
    dma = pltpu.SemaphoreType.DMA
    scratch = [
        pltpu.VMEM((NBUF, QC, nmu, basis), BF16),
        pltpu.VMEM((basis, no), BF16),
        pltpu.VMEM((rows // BLK, basis, no), BF16),
        pltpu.VMEM((lanes, QC * nmu, 128), F32),
        pltpu.VMEM((lanes, QC * nmu, 128), F32),
        pltpu.VMEM((NY, rows, kq), BF16),
        pltpu.VMEM((NX, rows, kq), BF16),
        pltpu.VMEM((nmu, NX, rows, no), BF16),
        pltpu.VMEM((nmu, rows, no), BF16),
        pltpu.VMEM((2, nmu, rows, no), BF16),
        pltpu.VMEM((nmu, rows, no), BF16),
        pltpu.VMEM((2, nmu, rows, no), BF16),
        pltpu.VMEM((lanes, rows * nmu, 128), F32),
        pltpu.VMEM((rows, nmu, no), BF16),
        pltpu.VMEM((2, 3, UNIT, 2 * rows, no), F32),
        pltpu.VMEM((no, no), F32),
        pltpu.VMEM((no // 2, no), F32),
        pltpu.VMEM((ncol, chunk, no), F32),
        pltpu.VMEM((ncol, chunk, no), F32),
        pltpu.VMEM((nrow // 2, chunk, no), F32),
        pltpu.VMEM((ncol, chunk, no), F32),
        pltpu.VMEM((ncol, chunk, no), F32),
        dma((NBUF,)),
        dma,
        dma,
        dma((NY - 1,)),
        dma((NY - 1,)),
        dma((NY - 1, nrow // 2 - 1)),
        dma((NY - 1, nrow // 2 - 1)),
        dma((NY - 1, nrow // 2)),
        dma((NY - 1, nrow // 2)),
        dma((2, 2, nmu // 2 // UNIT, 2)),
        dma((2, 2, nmu // 2 // UNIT, 2)),
        dma((2, 2, nmu // 2 // UNIT)),
        dma((2, 2, nmu // 2 // UNIT)),
        dma((2, 2, nmu // 2 // UNIT)),
        dma((2, 2, nmu // 2 // UNIT)),
        dma((2, nmu)),
        dma((2, nmu)),
        dma,
        dma,
        dma((ncol,)),
        dma((ncol,)),
        dma((nrow // 2,)),
        dma((nrow // 2,)),
        dma((ncol,)),
        dma((ncol,)),
        dma,
        dma,
        dma,
    ]
    anywhere = pl.BlockSpec(memory_space=pl.ANY)
    flops = 2 * rows * nmu * no * (basis + ncol * rows + no)
    return pl.pallas_call(
        functools.partial(kernel, dims),
        out_shape=(
            pltpu.VMEM((rows, nmu, no), BF16),
            pltpu.VMEM((no, no), F32),
        ),
        in_specs=[
            anywhere,
            pl.BlockSpec(memory_space=pltpu.SMEM),
            anywhere,
            anywhere,
        ],
        out_specs=(anywhere, pl.BlockSpec(memory_space=pltpu.VMEM)),
        scratch_shapes=scratch,
        compiler_params=pltpu.CompilerParams(
            collective_id=0, has_side_effects=True, vmem_limit_bytes=58 * 1024 * 1024
        ),
        cost_estimate=pl.CostEstimate(
            flops=flops, bytes_accessed=2 * rows * nmu * (basis + no), transcendentals=0
        ),
    )(integrals, occupancy.T, coeffs, metric)


def solution(mesh):
    placed = (P("col", "row", None), P(), P(), P("col", None))
    return jax.shard_map(
        functools.partial(on_device, mesh.shape["col"], mesh.shape["row"]),
        mesh=mesh,
        in_specs=placed,
        out_specs=(P("col", "row", None), P()),
        check_vma=False,
    )
```

```python
import functools

import jax
import jax.numpy as jnp
from jax import lax
from jax.experimental import pallas as pl
from jax.experimental.pallas import tpu as pltpu
from jax.sharding import PartitionSpec as P

BLK = 128
NX = 4
NY = 4
QC = 32
UNIT = 2
AHEAD = 2
LAG = 1
NBUF = 4
OPP, RIGHT, LEFT, OWN = range(4)
MESH = pl.DeviceIdType.MESH
F32 = jnp.float32
BF16 = jnp.bfloat16


def kernel(
    dims, integrals, occupancy, coeffs, metric, fitted, pair,
    ibuf, cbuf, cmask, stage_a, stage_b, mb, mbt, hbuf, opp_out, side_out, opp_in, side_in,
    rows_f32, out_bf16, pbuf, pair_acc, red0, mine, red1, red2, red3, red4,
    in_sem, c_sem, m_loc, m_send, m_recv, m2_send, m2_recv, m3_send, m3_recv,
    ag_send, ag_recv, fw_send, fw_recv, op_send, op_recv, sd_send, sd_recv,
    r0_send, r0_recv, r1_send, r1_recv, r2_send, r2_recv, r3_send, r3_recv,
    r4_send, r4_recv, out_sem,
):
    ncol, nrow, rows, nmu, basis, no, scale = dims
    half = rows // 2
    kq = NX * rows
    per_set = nmu // 2
    nset = per_set // UNIT
    nz = nrow // 2
    row = lax.axis_index("row")
    sib = row + 1 - 2 * lax.rem(row, 2)
    col = lax.axis_index("col")
    x = lax.rem(col, NX)
    y = lax.div(col, NX)
    nab = rows // BLK
    nch = rows // QC

    def col_x(d):
        return y * NX + lax.rem(x + d, NX)

    def col_y(d):
        return lax.rem(y + d, NY) * NX + x

    ag_to = ((col_x(1), col_x(NX - 1)), (col_y(1), col_y(NY - 1)))
    rs_to = (ag_to[1], ag_to[0])
    at_x = tuple(lax.rem(x + d, NX) for d in (0, NX - 1, 1, 2))
    held = (at_x, (OWN, LEFT, RIGHT, OPP))

    def in_copy(ch):
        q = pl.ds(ch * QC, QC)
        slot = lax.rem(ch, NBUF)
        return pltpu.make_async_copy(integrals.at[q], ibuf.at[slot], in_sem.at[slot])

    c_copy = pltpu.make_async_copy(coeffs, cbuf, c_sem)
    c_copy.start()

    @pl.loop(0, NBUF)
    def _(ch):
        in_copy(ch).start()

    def m_own():
        src = metric.at[:, pl.ds(pl.multiple_of(y * kq, 128), kq)]
        return pltpu.make_async_copy(src, mb.at[OWN], m_loc)

    m_own().start()

    barrier = pltpu.get_barrier_semaphore()

    @pl.loop(1, ncol)
    def _(d):
        pl.semaphore_signal(
            barrier, inc=1, device_id=(row, lax.rem(col + d, ncol)), device_id_type=MESH
        )

    @pl.loop(1, nrow)
    def _(d):
        pl.semaphore_signal(
            barrier, inc=1, device_id=(lax.rem(row + d, nrow), col), device_id_type=MESH
        )

    slot_of = {1: RIGHT, 2: OPP, 3: LEFT}
    share = rows // nrow

    def rows_of(r):
        return pl.ds(pl.multiple_of(r * share, 16), share)

    def m_copy(d):
        yd = lax.rem(y + d, NY)
        return pltpu.make_async_remote_copy(
            src_ref=metric.at[rows_of(row), pl.ds(pl.multiple_of(yd * kq, 128), kq)],
            dst_ref=mb.at[slot_of[NY - d], rows_of(row)],
            send_sem=m_send.at[d - 1],
            recv_sem=m_recv.at[NY - d - 1],
            device_id=(row, col_y(d)),
            device_id_type=MESH,
        )

    def m_landed(s):
        return pltpu.make_async_remote_copy(
            src_ref=metric.at[rows_of(row), pl.ds(0, kq)],
            dst_ref=mb.at[slot_of[s], rows_of(row)],
            send_sem=m_send.at[s - 1],
            recv_sem=m_recv.at[s - 1],
            device_id=(row, col_y(s)),
            device_id_type=MESH,
        )

    def along_z(d):
        return lax.rem(row + 2 * d, nrow)

    def m_share(s, d):
        blk = mb.at[slot_of[s], rows_of(row)]
        return pltpu.make_async_remote_copy(
            src_ref=blk,
            dst_ref=blk,
            send_sem=m2_send.at[s - 1, d - 1],
            recv_sem=m2_recv.at[s - 1, nz - d - 1],
            device_id=(along_z(d), col),
            device_id_type=MESH,
        )

    def m_shared(s, d):
        blk = mb.at[slot_of[s], rows_of(along_z(d))]
        return pltpu.make_async_remote_copy(
            src_ref=blk,
            dst_ref=blk,
            send_sem=m2_send.at[s - 1, d - 1],
            recv_sem=m2_recv.at[s - 1, d - 1],
            device_id=(along_z(d), col),
            device_id_type=MESH,
        )

    def m_pass(s, d, mine=True):
        src = along_z(d) if mine else lax.rem(sib + 2 * d, nrow)
        blk = mb.at[slot_of[s], rows_of(src)]
        return pltpu.make_async_remote_copy(
            src_ref=blk,
            dst_ref=blk,
            send_sem=m3_send.at[s - 1, d],
            recv_sem=m3_recv.at[s - 1, d],
            device_id=(sib, col),
            device_id_type=MESH,
        )

    c_copy.wait()
    for ab in range(nab):

        @pl.loop(0, basis // BLK, unroll=4)
        def _(nb):
            on = jnp.full((BLK, no), occupancy[nb, col * nab + ab], jnp.int32) > 0
            at = pl.ds(pl.multiple_of(nb * BLK, BLK), BLK)
            kept = jnp.where(on, cbuf[at, :].astype(F32), 0.0)
            cmask[ab, at, :] = kept.astype(BF16)

    pl.semaphore_wait(barrier, ncol + nrow - 2)

    for d in (2, 1, 3):
        m_copy(d).start()

    def transform(ch, ab, to):
        rowsin = ibuf[lax.rem(ch, NBUF)].reshape(QC * nmu, basis)
        res = jnp.dot(rowsin, cmask[ab], preferred_element_type=F32)
        for h in range(no // 128):
            to[h] = res[:, h * 128 : (h + 1) * 128]

    def relayout(ch, frm):
        q0 = pl.multiple_of(ch * QC, QC)
        for mu in range(nmu):
            own = held[mu // per_set][0]
            for h in range(no // 128):
                got = frm[h, pl.ds(mu, QC, stride=nmu), :]
                hbuf[mu, own, pl.ds(q0, QC), h * 128 : (h + 1) * 128] = got.astype(BF16)

    def mus(st, k):
        return pl.ds(st * per_set + k * UNIT, UNIT)

    def ag_copy(st, side, k, hf, blk=None, to=None):
        part_rows = pl.ds(hf * half, half)
        src = held[st][0] if blk is None else blk
        dst = (at_x[0], (LEFT, RIGHT)[side])[st] if to is None else to
        return pltpu.make_async_remote_copy(
            src_ref=hbuf.at[mus(st, k), src, part_rows],
            dst_ref=hbuf.at[mus(st, k), dst, part_rows],
            send_sem=ag_send.at[st, side, k, hf],
            recv_sem=ag_recv.at[st, side, k, hf],
            device_id=(row, ag_to[st][side]),
            device_id_type=MESH,
        )

    def ag_wait(st, side, k, hf):
        blk = held[st][1 + side]
        ag_copy(st, side, k, hf, blk, blk).wait_recv()

    def fw_copy(st, side, k, blk=None, to=None):
        part_rows = pl.ds(side * half, half)
        src = held[st][1 + side] if blk is None else blk
        dst = (at_x[1 + side], OPP)[st] if to is None else to
        return pltpu.make_async_remote_copy(
            src_ref=hbuf.at[mus(st, k), src, part_rows],
            dst_ref=hbuf.at[mus(st, k), dst, part_rows],
            send_sem=fw_send.at[st, side, k],
            recv_sem=fw_recv.at[st, side, k],
            device_id=(row, ag_to[st][side]),
            device_id_type=MESH,
        )

    def fw_wait(st, side, k):
        blk = held[st][3]
        fw_copy(st, side, k, blk, blk).wait_recv()

    def op_copy(st, side, k):
        part_rows = pl.ds(side * half, half)
        return pltpu.make_async_remote_copy(
            src_ref=opp_out.at[mus(st, k), part_rows],
            dst_ref=opp_in.at[mus(st, k), part_rows],
            send_sem=op_send.at[st, side, k],
            recv_sem=op_recv.at[st, side, k],
            device_id=(row, rs_to[st][side]),
            device_id_type=MESH,
        )

    def sd_copy(st, side, mu):
        return pltpu.make_async_remote_copy(
            src_ref=side_out.at[side, mu],
            dst_ref=side_in.at[side, mu],
            send_sem=sd_send.at[side, mu],
            recv_sem=sd_recv.at[side, mu],
            device_id=(row, rs_to[st][side]),
            device_id_type=MESH,
        )

    def ag_start(st, k):
        for step in range(2):
            ag_copy(st, 0, k, step).start()
            ag_copy(st, 1, k, 1 - step).start()

    def forward(st, k):
        for side in range(2):
            ag_wait(st, side, k, side)
            fw_copy(st, side, k).start()

    def product(st, k):
        block = (mb, mbt)[st]
        for side in range(2):
            ag_wait(st, side, k, 1 - side)
            fw_wait(st, side, k)

        @pl.loop(0, UNIT)
        def _(m):
            mu = st * per_set + k * UNIT + m
            full = hbuf[mu].reshape(kq, no)
            got = jnp.dot(block[...].reshape(NY * rows, kq), full, preferred_element_type=F32)
            opp_out[mu] = got[:rows].astype(BF16)
            for side in range(2):
                at = (1 + side) * rows
                first = got[at : at + half]
                second = got[at + half : at + rows]
                plain = pl.ds((1 - side) * half, half)
                side_out[side, mu, plain] = (second, first)[side].astype(BF16)
                pbuf[st, lax.rem(k, 3), m, pl.ds(side * half, half)] = (first, second)[side]
            pbuf[st, lax.rem(k, 3), m, pl.ds(rows, rows)] = got[3 * rows :]

        op_copy(st, 0, k).start()
        op_copy(st, 1, k).start()

    def sides(k):
        for m in range(UNIT):
            for st in range(2):
                mu = st * per_set + k * UNIT + m
                for side in range(2):
                    if m == 0:
                        op_copy(st, side, k).wait_recv()
                    at = pl.ds(side * half, half)
                    side_out[side, mu, at] = (
                        pbuf[st, lax.rem(k, 3), m, at] + opp_in[mu, at].astype(F32)
                    ).astype(BF16)
                    sd_copy(st, side, mu).start()

    pair_acc[...] = jnp.zeros_like(pair_acc)

    def finish(k):
        @pl.loop(0, UNIT)
        def _(m):
            pairs = []
            for st in range(2):
                for side in range(2):
                    sd_copy(st, side, st * per_set + k * UNIT + m).wait_recv()
            for st in range(2):
                mu = st * per_set + k * UNIT + m
                own = pbuf[st, lax.rem(k, 3), m, pl.ds(rows, rows)]
                total = own + side_in[0, mu].astype(F32) + side_in[1, mu].astype(F32)
                done = total.astype(BF16)
                back = done.astype(F32)
                for h in range(no // 128):
                    at = pl.ds(mu, rows, stride=nmu)
                    rows_f32[h, at, :] = back[:, h * 128 : (h + 1) * 128]
                pairs.append(done)
            both = jnp.concatenate(pairs, axis=0)
            pair_acc[...] += lax.dot_general(
                both, both, (((0,), (0,)), ((), ())), preferred_element_type=F32
            )

    quarter = rows // 4

    def send_quarter(qt):
        part_rows = pl.ds(pl.multiple_of(qt * quarter, quarter), quarter)
        for k in range(AHEAD):
            for st in range(2):
                for side in range(2):
                    pltpu.make_async_remote_copy(
                        src_ref=hbuf.at[mus(st, k), held[st][0], part_rows],
                        dst_ref=hbuf.at[
                            mus(st, k), (at_x[0], (LEFT, RIGHT)[side])[st], part_rows
                        ],
                        send_sem=ag_send.at[st, side, k, lax.div(qt, 2)],
                        recv_sem=ag_recv.at[st, side, k, lax.div(qt, 2)],
                        device_id=(row, ag_to[st][side]),
                        device_id_type=MESH,
                    ).start()

    stage_b[...] = jnp.zeros_like(stage_b)

    @pl.loop(0, nch // 2)
    def _(j):
        ch = 2 * j
        ab = lax.div(ch * QC, BLK)
        in_copy(ch).wait()
        in_copy(ch + 1).wait()
        transform(ch, ab, stage_a)
        relayout(lax.max(ch - 1, 0), stage_b)

        @pl.when(j >= 1)
        def _():
            send_quarter(j - 1)

        @pl.when(j == 1)
        def _():
            for s in (2, 1, 3):
                m_landed(s).wait_recv()
                for d in (2, 1, 3):
                    m_share(s, d).start()
                m_pass(s, 0).start()

        transform(ch + 1, ab, stage_b)
        relayout(ch, stage_a)

        @pl.when(ch + NBUF < nch)
        def _():
            in_copy(ch + NBUF).start()
            in_copy(ch + NBUF + 1).start()

    relayout(nch - 1, stage_b)
    send_quarter(nch // 2 - 1)

    def metric_sent():
        for s in range(1, NY):
            m_copy(s).wait_send()
            for d in range(nz):
                m_pass(s, d).wait_send()
            for d in range(1, nz):
                m_share(s, d).wait_send()

    def sent_early(k):
        for st in range(2):
            for side in range(2):
                for hf in range(2):
                    ag_copy(st, side, k, hf).wait_send()
                fw_copy(st, side, k).wait_send()
                op_copy(st, side, k).wait_send()

    def sent_late(k):
        for st in range(2):
            for side in range(2):
                for m in range(UNIT):
                    sd_copy(st, side, st * per_set + k * UNIT + m).wait_send()

    def metric_ready():
        for d in range(nz):
            for s in (2, 1, 3):
                m_pass(s, d, False).wait_recv()

    def transpose_metric(begin, end):
        offs = {OPP: 2, RIGHT: 1, LEFT: NX - 1, OWN: 0}
        for to, d in offs.items():
            at = pl.ds(pl.multiple_of(lax.rem(x + d, NX) * rows, 128), rows)

            @pl.loop(begin, end)
            def _(s):
                mbt[to, :, pl.ds(pl.multiple_of(s * rows, 128), rows)] = mb[s, :, at].T

    @pl.loop(0, nset + LAG + 2)
    def _(k):
        @pl.when(k < nset)
        def _():
            forward(0, k)
            forward(1, k)

        @pl.when(k + AHEAD < nset)
        def _():
            ag_start(0, k + AHEAD)
            ag_start(1, k + AHEAD)

        @pl.when(k == 0)
        def _():
            m_own().wait()
            transpose_metric(OWN, OWN + 1)
            for s in (2, 1, 3):
                for d in (1, 3, 2):
                    m_shared(s, d).wait_recv()
                    m_pass(s, d).start()

        @pl.when((k >= LAG) & (k < nset + LAG))
        def _():
            @pl.when(k == LAG)
            def _():
                metric_ready()

            product(0, k - LAG)

            @pl.when(k == LAG)
            def _():
                transpose_metric(OPP, OWN)

            product(1, k - LAG)

        @pl.when((k >= LAG + 1) & (k < nset + LAG + 1))
        def _():
            sides(k - LAG - 1)
            sent_early(k - LAG - 1)

        @pl.when(k == LAG + 1)
        def _():
            metric_sent()

        @pl.when(k >= LAG + 2)
        def _():
            finish(k - LAG - 2)

        @pl.when((k >= LAG + 2) & (k < nset + LAG + 1))
        def _():
            sent_late(k - LAG - 2)

    chunk = no // 2 // ncol
    core = lax.rem(row, 2)
    mid = no // 2
    mine_at = pl.ds(pl.multiple_of(core * mid, 8), mid)
    theirs_at = pl.ds(pl.multiple_of((1 - core) * mid, 8), mid)

    r0_copy = pltpu.make_async_remote_copy(
        src_ref=pair_acc.at[theirs_at],
        dst_ref=red0,
        send_sem=r0_send,
        recv_sem=r0_recv,
        device_id=(sib, col),
        device_id_type=MESH,
    )
    r0_copy.start()

    def r1_copy(d):
        to = lax.rem(col + d, ncol)
        return pltpu.make_async_remote_copy(
            src_ref=mine.at[to],
            dst_ref=red1.at[col],
            send_sem=r1_send.at[d],
            recv_sem=r1_recv.at[col],
            device_id=(row, to),
            device_id_type=MESH,
        )

    def r1_landed(src):
        return pltpu.make_async_remote_copy(
            src_ref=mine.at[src],
            dst_ref=red1.at[src],
            send_sem=r1_send.at[0],
            recv_sem=r1_recv.at[src],
            device_id=(row, src),
            device_id_type=MESH,
        )

    def r2_copy(d):
        z = lax.div(row, 2)
        return pltpu.make_async_remote_copy(
            src_ref=red2.at[z],
            dst_ref=red2.at[z],
            send_sem=r2_send.at[d],
            recv_sem=r2_recv.at[z],
            device_id=(along_z(d), col),
            device_id_type=MESH,
        )

    def r2_landed(d):
        z = lax.div(along_z(d), 2)
        return pltpu.make_async_remote_copy(
            src_ref=red2.at[z],
            dst_ref=red2.at[z],
            send_sem=r2_send.at[d],
            recv_sem=r2_recv.at[z],
            device_id=(along_z(d), col),
            device_id_type=MESH,
        )

    def r3_copy(d):
        to = lax.rem(col + d, ncol)
        return pltpu.make_async_remote_copy(
            src_ref=red3.at[col],
            dst_ref=red3.at[col],
            send_sem=r3_send.at[d],
            recv_sem=r3_recv.at[col],
            device_id=(row, to),
            device_id_type=MESH,
        )

    def r3_landed(src):
        return pltpu.make_async_remote_copy(
            src_ref=red3.at[src],
            dst_ref=red3.at[src],
            send_sem=r3_send.at[0],
            recv_sem=r3_recv.at[src],
            device_id=(row, src),
            device_id_type=MESH,
        )

    def lay_out(begin, end):
        @pl.loop(begin, end)
        def _(ch):
            at = pl.ds(pl.multiple_of(ch * QC * nmu, QC), QC * nmu)
            for h in range(no // 128):
                out_bf16[pl.ds(ch * QC, QC), :, h * 128 : (h + 1) * 128] = (
                    rows_f32[h, at, :].astype(BF16).reshape(QC, nmu, 128)
                )

    lay_out(0, nch // 4)
    r0_copy.wait_recv()
    mine[...] = (pair_acc[mine_at] + red0[...]).reshape(ncol, chunk, no)

    @pl.loop(1, ncol, unroll=5)
    def _(d):
        r1_copy(d).start()

    red1[col] = mine[col]

    lay_out(nch // 4, nch)
    sent_late(nset - 1)

    out_copy = pltpu.make_async_copy(out_bf16, fitted, out_sem)
    out_copy.start()

    @pl.loop(1, ncol)
    def _(d):
        r1_landed(lax.rem(col + d, ncol)).wait_recv()

    total = red1[0]
    for c in range(1, ncol):
        total = total + red1[c]
    red2[lax.div(row, 2)] = total
    for d in (2, 1, 3):
        r2_copy(d).start()
    for d in (1, 3, 2):
        r2_landed(d).wait_recv()

    total = red2[0]
    for z in range(1, nz):
        total = total + red2[z]
    red3[col] = total * F32(scale)

    @pl.loop(1, ncol, unroll=5)
    def _(d):
        r3_copy(d).start()

    @pl.loop(1, ncol, unroll=5)
    def _(d):
        r3_landed(lax.rem(col + d, ncol)).wait_recv()

    r4_copy = pltpu.make_async_remote_copy(
        src_ref=red3,
        dst_ref=red4,
        send_sem=r4_send,
        recv_sem=r4_recv,
        device_id=(sib, col),
        device_id_type=MESH,
    )
    r4_copy.start()
    pair[mine_at] = red3[...].reshape(mid, no)

    r0_copy.wait_send()

    @pl.loop(1, ncol)
    def _(d):
        r1_copy(d).wait_send()
        r3_copy(d).wait_send()

    for d in range(1, nz):
        r2_copy(d).wait_send()

    r4_copy.wait_recv()
    pair[theirs_at] = red4[...].reshape(mid, no)
    r4_copy.wait_send()
    out_copy.wait()


def on_device(ncol, nrow, integrals, occupancy, coeffs, metric):
    rows, nmu, basis = integrals.shape
    no = coeffs.shape[1]
    kq = NX * rows
    chunk = no // 2 // ncol
    scale = 1.0 / (rows * ncol * nmu * nrow)
    dims = (ncol, nrow, rows, nmu, basis, no, scale)
    lanes = no // 128
    dma = pltpu.SemaphoreType.DMA
    scratch = [
        pltpu.VMEM((NBUF, QC, nmu, basis), BF16),
        pltpu.VMEM((basis, no), BF16),
        pltpu.VMEM((rows // BLK, basis, no), BF16),
        pltpu.VMEM((lanes, QC * nmu, 128), F32),
        pltpu.VMEM((lanes, QC * nmu, 128), F32),
        pltpu.VMEM((NY, rows, kq), BF16),
        pltpu.VMEM((NX, rows, kq), BF16),
        pltpu.VMEM((nmu, NX, rows, no), BF16),
        pltpu.VMEM((nmu, rows, no), BF16),
        pltpu.VMEM((2, nmu, rows, no), BF16),
        pltpu.VMEM((nmu, rows, no), BF16),
        pltpu.VMEM((2, nmu, rows, no), BF16),
        pltpu.VMEM((lanes, rows * nmu, 128), F32),
        pltpu.VMEM((rows, nmu, no), BF16),
        pltpu.VMEM((2, 3, UNIT, 2 * rows, no), F32),
        pltpu.VMEM((no, no), F32),
        pltpu.VMEM((no // 2, no), F32),
        pltpu.VMEM((ncol, chunk, no), F32),
        pltpu.VMEM((ncol, chunk, no), F32),
        pltpu.VMEM((nrow // 2, chunk, no), F32),
        pltpu.VMEM((ncol, chunk, no), F32),
        pltpu.VMEM((ncol, chunk, no), F32),
        dma((NBUF,)),
        dma,
        dma,
        dma((NY - 1,)),
        dma((NY - 1,)),
        dma((NY - 1, nrow // 2 - 1)),
        dma((NY - 1, nrow // 2 - 1)),
        dma((NY - 1, nrow // 2)),
        dma((NY - 1, nrow // 2)),
        dma((2, 2, nmu // 2 // UNIT, 2)),
        dma((2, 2, nmu // 2 // UNIT, 2)),
        dma((2, 2, nmu // 2 // UNIT)),
        dma((2, 2, nmu // 2 // UNIT)),
        dma((2, 2, nmu // 2 // UNIT)),
        dma((2, 2, nmu // 2 // UNIT)),
        dma((2, nmu)),
        dma((2, nmu)),
        dma,
        dma,
        dma((ncol,)),
        dma((ncol,)),
        dma((nrow // 2,)),
        dma((nrow // 2,)),
        dma((ncol,)),
        dma((ncol,)),
        dma,
        dma,
        dma,
    ]
    anywhere = pl.BlockSpec(memory_space=pl.ANY)
    flops = 2 * rows * nmu * no * (basis + ncol * rows + no)
    return pl.pallas_call(
        functools.partial(kernel, dims),
        out_shape=(
            pltpu.VMEM((rows, nmu, no), BF16),
            pltpu.VMEM((no, no), F32),
        ),
        in_specs=[
            anywhere,
            pl.BlockSpec(memory_space=pltpu.SMEM),
            anywhere,
            anywhere,
        ],
        out_specs=(anywhere, pl.BlockSpec(memory_space=pltpu.VMEM)),
        scratch_shapes=scratch,
        compiler_params=pltpu.CompilerParams(
            collective_id=0, has_side_effects=True, vmem_limit_bytes=58 * 1024 * 1024
        ),
        cost_estimate=pl.CostEstimate(
            flops=flops, bytes_accessed=2 * rows * nmu * (basis + no), transcendentals=0
        ),
    )(integrals, occupancy.T, coeffs, metric)


def solution(mesh):
    placed = (P("col", "row", None), P(), P(), P("col", None))
    return jax.shard_map(
        functools.partial(on_device, mesh.shape["col"], mesh.shape["row"]),
        mesh=mesh,
        in_specs=placed,
        out_specs=(P("col", "row", None), P()),
        check_vma=False,
    )
```

```python
import functools

import jax
import jax.numpy as jnp
from jax import lax
from jax.experimental import pallas as pl
from jax.experimental.pallas import tpu as pltpu
from jax.sharding import PartitionSpec as P

BLK = 128
NX = 4
NY = 4
QC = 32
UNIT = 2
AHEAD = 2
LAG = 1
NBUF = 4
OPP, RIGHT, LEFT, OWN = range(4)
MESH = pl.DeviceIdType.MESH
F32 = jnp.float32
BF16 = jnp.bfloat16


def kernel(
    dims, integrals, occupancy, coeffs, metric, fitted, pair,
    ibuf, cbuf, cmask, stage_a, stage_b, mb, mbt, hbuf, opp_out, side_out, opp_in, side_in,
    rows_f32, out_bf16, pbuf, pair_acc, red0, mine, red1, red2, red3, red4,
    in_sem, c_sem, m_loc, m_send, m_recv, m2_send, m2_recv, m3_send, m3_recv,
    ag_send, ag_recv, fw_send, fw_recv, op_send, op_recv, sd_send, sd_recv,
    r0_send, r0_recv, r1_send, r1_recv, r2_send, r2_recv, r3_send, r3_recv,
    r4_send, r4_recv, out_sem,
):
    ncol, nrow, rows, nmu, basis, no, scale = dims
    half = rows // 2
    kq = NX * rows
    per_set = nmu // 2
    nset = per_set // UNIT
    nz = nrow // 2
    row = lax.axis_index("row")
    sib = row + 1 - 2 * lax.rem(row, 2)
    col = lax.axis_index("col")
    x = lax.rem(col, NX)
    y = lax.div(col, NX)
    nab = rows // BLK
    nch = rows // QC

    def col_x(d):
        return y * NX + lax.rem(x + d, NX)

    def col_y(d):
        return lax.rem(y + d, NY) * NX + x

    ag_to = ((col_x(1), col_x(NX - 1)), (col_y(1), col_y(NY - 1)))
    rs_to = (ag_to[1], ag_to[0])
    at_x = tuple(lax.rem(x + d, NX) for d in (0, NX - 1, 1, 2))
    held = (at_x, (OWN, LEFT, RIGHT, OPP))

    def in_copy(ch):
        q = pl.ds(ch * QC, QC)
        slot = lax.rem(ch, NBUF)
        return pltpu.make_async_copy(integrals.at[q], ibuf.at[slot], in_sem.at[slot])

    c_copy = pltpu.make_async_copy(coeffs, cbuf, c_sem)
    c_copy.start()

    @pl.loop(0, NBUF)
    def _(ch):
        in_copy(ch).start()

    def m_own():
        src = metric.at[:, pl.ds(pl.multiple_of(y * kq, 128), kq)]
        return pltpu.make_async_copy(src, mb.at[OWN], m_loc)

    m_own().start()

    barrier = pltpu.get_barrier_semaphore()

    @pl.loop(1, ncol)
    def _(d):
        pl.semaphore_signal(
            barrier, inc=1, device_id=(row, lax.rem(col + d, ncol)), device_id_type=MESH
        )

    @pl.loop(1, nrow)
    def _(d):
        pl.semaphore_signal(
            barrier, inc=1, device_id=(lax.rem(row + d, nrow), col), device_id_type=MESH
        )

    slot_of = {1: RIGHT, 2: OPP, 3: LEFT}
    share = rows // nrow

    def rows_of(r):
        return pl.ds(pl.multiple_of(r * share, 16), share)

    def m_copy(d):
        yd = lax.rem(y + d, NY)
        return pltpu.make_async_remote_copy(
            src_ref=metric.at[rows_of(row), pl.ds(pl.multiple_of(yd * kq, 128), kq)],
            dst_ref=mb.at[slot_of[NY - d], rows_of(row)],
            send_sem=m_send.at[d - 1],
            recv_sem=m_recv.at[NY - d - 1],
            device_id=(row, col_y(d)),
            device_id_type=MESH,
        )

    def m_landed(s):
        return pltpu.make_async_remote_copy(
            src_ref=metric.at[rows_of(row), pl.ds(0, kq)],
            dst_ref=mb.at[slot_of[s], rows_of(row)],
            send_sem=m_send.at[s - 1],
            recv_sem=m_recv.at[s - 1],
            device_id=(row, col_y(s)),
            device_id_type=MESH,
        )

    def along_z(d):
        return lax.rem(row + 2 * d, nrow)

    def m_share(s, d):
        blk = mb.at[slot_of[s], rows_of(row)]
        return pltpu.make_async_remote_copy(
            src_ref=blk,
            dst_ref=blk,
            send_sem=m2_send.at[s - 1, d - 1],
            recv_sem=m2_recv.at[s - 1, nz - d - 1],
            device_id=(along_z(d), col),
            device_id_type=MESH,
        )

    def m_shared(s, d):
        blk = mb.at[slot_of[s], rows_of(along_z(d))]
        return pltpu.make_async_remote_copy(
            src_ref=blk,
            dst_ref=blk,
            send_sem=m2_send.at[s - 1, d - 1],
            recv_sem=m2_recv.at[s - 1, d - 1],
            device_id=(along_z(d), col),
            device_id_type=MESH,
        )

    def m_pass(s, d, mine=True):
        src = along_z(d) if mine else lax.rem(sib + 2 * d, nrow)
        blk = mb.at[slot_of[s], rows_of(src)]
        return pltpu.make_async_remote_copy(
            src_ref=blk,
            dst_ref=blk,
            send_sem=m3_send.at[s - 1, d],
            recv_sem=m3_recv.at[s - 1, d],
            device_id=(sib, col),
            device_id_type=MESH,
        )

    c_copy.wait()
    for ab in range(nab):

        @pl.loop(0, basis // BLK, unroll=4)
        def _(nb):
            on = jnp.full((BLK, no), occupancy[nb, col * nab + ab], jnp.int32) > 0
            at = pl.ds(pl.multiple_of(nb * BLK, BLK), BLK)
            kept = jnp.where(on, cbuf[at, :].astype(F32), 0.0)
            cmask[ab, at, :] = kept.astype(BF16)

    pl.semaphore_wait(barrier, ncol + nrow - 2)

    for d in (2, 1, 3):
        m_copy(d).start()

    def transform(ch, ab, to):
        rowsin = ibuf[lax.rem(ch, NBUF)].reshape(QC * nmu, basis)
        res = jnp.dot(rowsin, cmask[ab], preferred_element_type=F32)
        for h in range(no // 128):
            to[h] = res[:, h * 128 : (h + 1) * 128]

    def relayout(ch, frm):
        q0 = pl.multiple_of(ch * QC, QC)
        for mu in range(nmu):
            own = held[mu // per_set][0]
            for h in range(no // 128):
                got = frm[h, pl.ds(mu, QC, stride=nmu), :]
                hbuf[mu, own, pl.ds(q0, QC), h * 128 : (h + 1) * 128] = got.astype(BF16)

    def mus(st, k):
        return pl.ds(st * per_set + k * UNIT, UNIT)

    def ag_copy(st, side, k, hf, blk=None, to=None):
        part_rows = pl.ds(hf * half, half)
        src = held[st][0] if blk is None else blk
        dst = (at_x[0], (LEFT, RIGHT)[side])[st] if to is None else to
        return pltpu.make_async_remote_copy(
            src_ref=hbuf.at[mus(st, k), src, part_rows],
            dst_ref=hbuf.at[mus(st, k), dst, part_rows],
            send_sem=ag_send.at[st, side, k, hf],
            recv_sem=ag_recv.at[st, side, k, hf],
            device_id=(row, ag_to[st][side]),
            device_id_type=MESH,
        )

    def ag_wait(st, side, k, hf):
        blk = held[st][1 + side]
        ag_copy(st, side, k, hf, blk, blk).wait_recv()

    def fw_copy(st, side, k, blk=None, to=None):
        part_rows = pl.ds(side * half, half)
        src = held[st][1 + side] if blk is None else blk
        dst = (at_x[1 + side], OPP)[st] if to is None else to
        return pltpu.make_async_remote_copy(
            src_ref=hbuf.at[mus(st, k), src, part_rows],
            dst_ref=hbuf.at[mus(st, k), dst, part_rows],
            send_sem=fw_send.at[st, side, k],
            recv_sem=fw_recv.at[st, side, k],
            device_id=(row, ag_to[st][side]),
            device_id_type=MESH,
        )

    def fw_wait(st, side, k):
        blk = held[st][3]
        fw_copy(st, side, k, blk, blk).wait_recv()

    def op_copy(st, side, k):
        part_rows = pl.ds(side * half, half)
        return pltpu.make_async_remote_copy(
            src_ref=opp_out.at[mus(st, k), part_rows],
            dst_ref=opp_in.at[mus(st, k), part_rows],
            send_sem=op_send.at[st, side, k],
            recv_sem=op_recv.at[st, side, k],
            device_id=(row, rs_to[st][side]),
            device_id_type=MESH,
        )

    def sd_copy(st, side, mu):
        return pltpu.make_async_remote_copy(
            src_ref=side_out.at[side, mu],
            dst_ref=side_in.at[side, mu],
            send_sem=sd_send.at[side, mu],
            recv_sem=sd_recv.at[side, mu],
            device_id=(row, rs_to[st][side]),
            device_id_type=MESH,
        )

    def ag_start(st, k):
        for step in range(2):
            ag_copy(st, 0, k, step).start()
            ag_copy(st, 1, k, 1 - step).start()

    def forward(st, k):
        for side in range(2):
            ag_wait(st, side, k, side)
            fw_copy(st, side, k).start()

    def product(st, k):
        block = (mb, mbt)[st]
        for side in range(2):
            ag_wait(st, side, k, 1 - side)
            fw_wait(st, side, k)

        base = st * per_set + k * UNIT
        full = jnp.concatenate([hbuf[base + m].reshape(kq, no) for m in range(UNIT)], axis=1)
        got = jnp.dot(block[...].reshape(NY * rows, kq), full, preferred_element_type=F32)
        for m in range(UNIT):
            mu = base + m
            lanes = slice(m * no, (m + 1) * no)
            opp_out[mu] = got[:rows, lanes].astype(BF16)
            for side in range(2):
                at = (1 + side) * rows
                first = got[at : at + half, lanes]
                second = got[at + half : at + rows, lanes]
                plain = pl.ds((1 - side) * half, half)
                side_out[side, mu, plain] = (second, first)[side].astype(BF16)
                pbuf[st, lax.rem(k, 3), m, pl.ds(side * half, half)] = (first, second)[side]
            pbuf[st, lax.rem(k, 3), m, pl.ds(rows, rows)] = got[3 * rows :, lanes]

        op_copy(st, 0, k).start()
        op_copy(st, 1, k).start()

    def sides(k):
        for m in range(UNIT):
            for st in range(2):
                mu = st * per_set + k * UNIT + m
                for side in range(2):
                    if m == 0:
                        op_copy(st, side, k).wait_recv()
                    at = pl.ds(side * half, half)
                    side_out[side, mu, at] = (
                        pbuf[st, lax.rem(k, 3), m, at] + opp_in[mu, at].astype(F32)
                    ).astype(BF16)
                    sd_copy(st, side, mu).start()

    pair_acc[...] = jnp.zeros_like(pair_acc)

    def finish(k):
        @pl.loop(0, UNIT)
        def _(m):
            pairs = []
            for st in range(2):
                for side in range(2):
                    sd_copy(st, side, st * per_set + k * UNIT + m).wait_recv()
            for st in range(2):
                mu = st * per_set + k * UNIT + m
                own = pbuf[st, lax.rem(k, 3), m, pl.ds(rows, rows)]
                total = own + side_in[0, mu].astype(F32) + side_in[1, mu].astype(F32)
                done = total.astype(BF16)
                back = done.astype(F32)
                for h in range(no // 128):
                    at = pl.ds(mu, rows, stride=nmu)
                    rows_f32[h, at, :] = back[:, h * 128 : (h + 1) * 128]
                pairs.append(done)
            both = jnp.concatenate(pairs, axis=0)
            pair_acc[...] += lax.dot_general(
                both, both, (((0,), (0,)), ((), ())), preferred_element_type=F32
            )

    quarter = rows // 4

    def send_quarter(qt):
        part_rows = pl.ds(pl.multiple_of(qt * quarter, quarter), quarter)
        for k in range(AHEAD):
            for st in range(2):
                for side in range(2):
                    pltpu.make_async_remote_copy(
                        src_ref=hbuf.at[mus(st, k), held[st][0], part_rows],
                        dst_ref=hbuf.at[
                            mus(st, k), (at_x[0], (LEFT, RIGHT)[side])[st], part_rows
                        ],
                        send_sem=ag_send.at[st, side, k, lax.div(qt, 2)],
                        recv_sem=ag_recv.at[st, side, k, lax.div(qt, 2)],
                        device_id=(row, ag_to[st][side]),
                        device_id_type=MESH,
                    ).start()

    stage_b[...] = jnp.zeros_like(stage_b)

    @pl.loop(0, nch // 2)
    def _(j):
        ch = 2 * j
        ab = lax.div(ch * QC, BLK)
        in_copy(ch).wait()
        in_copy(ch + 1).wait()
        transform(ch, ab, stage_a)
        relayout(lax.max(ch - 1, 0), stage_b)

        @pl.when(j >= 1)
        def _():
            send_quarter(j - 1)

        @pl.when(j == 1)
        def _():
            for s in (2, 1, 3):
                m_landed(s).wait_recv()
                for d in (2, 1, 3):
                    m_share(s, d).start()
                m_pass(s, 0).start()

        transform(ch + 1, ab, stage_b)
        relayout(ch, stage_a)

        @pl.when(ch + NBUF < nch)
        def _():
            in_copy(ch + NBUF).start()
            in_copy(ch + NBUF + 1).start()

    relayout(nch - 1, stage_b)
    send_quarter(nch // 2 - 1)

    def metric_sent():
        for s in range(1, NY):
            m_copy(s).wait_send()
            for d in range(nz):
                m_pass(s, d).wait_send()
            for d in range(1, nz):
                m_share(s, d).wait_send()

    def sent_early(k):
        for st in range(2):
            for side in range(2):
                for hf in range(2):
                    ag_copy(st, side, k, hf).wait_send()
                fw_copy(st, side, k).wait_send()
                op_copy(st, side, k).wait_send()

    def sent_late(k):
        for st in range(2):
            for side in range(2):
                for m in range(UNIT):
                    sd_copy(st, side, st * per_set + k * UNIT + m).wait_send()

    def metric_ready():
        m_own().wait()
        for d in range(nz):
            for s in (2, 1, 3):
                m_pass(s, d, False).wait_recv()

    def transpose_metric():
        offs = {OPP: 2, RIGHT: 1, LEFT: NX - 1, OWN: 0}
        for to, d in offs.items():
            at = pl.ds(pl.multiple_of(lax.rem(x + d, NX) * rows, 128), rows)

            @pl.loop(0, NY)
            def _(s):
                mbt[to, :, pl.ds(pl.multiple_of(s * rows, 128), rows)] = mb[s, :, at].T

    @pl.loop(0, nset + LAG + 2)
    def _(k):
        @pl.when(k + AHEAD < nset)
        def _():
            ag_start(0, k + AHEAD)
            ag_start(1, k + AHEAD)

        @pl.when(k < nset)
        def _():
            forward(0, k)
            forward(1, k)

        @pl.when(k == 0)
        def _():
            for s in (2, 1, 3):
                for d in (1, 3, 2):
                    m_shared(s, d).wait_recv()
                    m_pass(s, d).start()

        @pl.when((k >= LAG) & (k < nset + LAG))
        def _():
            @pl.when(k == LAG)
            def _():
                metric_ready()

            product(0, k - LAG)

            @pl.when(k == LAG)
            def _():
                transpose_metric()

            product(1, k - LAG)

        @pl.when((k >= LAG + 1) & (k < nset + LAG + 1))
        def _():
            sides(k - LAG - 1)
            sent_early(k - LAG - 1)

        @pl.when(k == LAG + 1)
        def _():
            metric_sent()

        @pl.when(k >= LAG + 2)
        def _():
            finish(k - LAG - 2)

        @pl.when((k >= LAG + 2) & (k < nset + LAG + 1))
        def _():
            sent_late(k - LAG - 2)

    chunk = no // 2 // ncol
    core = lax.rem(row, 2)
    mid = no // 2
    mine_at = pl.ds(pl.multiple_of(core * mid, 8), mid)
    theirs_at = pl.ds(pl.multiple_of((1 - core) * mid, 8), mid)

    r0_copy = pltpu.make_async_remote_copy(
        src_ref=pair_acc.at[theirs_at],
        dst_ref=red0,
        send_sem=r0_send,
        recv_sem=r0_recv,
        device_id=(sib, col),
        device_id_type=MESH,
    )
    r0_copy.start()

    def r1_copy(d):
        to = lax.rem(col + d, ncol)
        return pltpu.make_async_remote_copy(
            src_ref=mine.at[to],
            dst_ref=red1.at[col],
            send_sem=r1_send.at[d],
            recv_sem=r1_recv.at[col],
            device_id=(row, to),
            device_id_type=MESH,
        )

    def r1_landed(src):
        return pltpu.make_async_remote_copy(
            src_ref=mine.at[src],
            dst_ref=red1.at[src],
            send_sem=r1_send.at[0],
            recv_sem=r1_recv.at[src],
            device_id=(row, src),
            device_id_type=MESH,
        )

    def r2_copy(d):
        z = lax.div(row, 2)
        return pltpu.make_async_remote_copy(
            src_ref=red2.at[z],
            dst_ref=red2.at[z],
            send_sem=r2_send.at[d],
            recv_sem=r2_recv.at[z],
            device_id=(along_z(d), col),
            device_id_type=MESH,
        )

    def r2_landed(d):
        z = lax.div(along_z(d), 2)
        return pltpu.make_async_remote_copy(
            src_ref=red2.at[z],
            dst_ref=red2.at[z],
            send_sem=r2_send.at[d],
            recv_sem=r2_recv.at[z],
            device_id=(along_z(d), col),
            device_id_type=MESH,
        )

    def r3_copy(d):
        to = lax.rem(col + d, ncol)
        return pltpu.make_async_remote_copy(
            src_ref=red3.at[col],
            dst_ref=red3.at[col],
            send_sem=r3_send.at[d],
            recv_sem=r3_recv.at[col],
            device_id=(row, to),
            device_id_type=MESH,
        )

    def r3_landed(src):
        return pltpu.make_async_remote_copy(
            src_ref=red3.at[src],
            dst_ref=red3.at[src],
            send_sem=r3_send.at[0],
            recv_sem=r3_recv.at[src],
            device_id=(row, src),
            device_id_type=MESH,
        )

    def lay_out(begin, end):
        @pl.loop(begin, end)
        def _(ch):
            at = pl.ds(pl.multiple_of(ch * QC * nmu, QC), QC * nmu)
            for h in range(no // 128):
                out_bf16[pl.ds(ch * QC, QC), :, h * 128 : (h + 1) * 128] = (
                    rows_f32[h, at, :].astype(BF16).reshape(QC, nmu, 128)
                )

    lay_out(0, nch // 4)
    r0_copy.wait_recv()
    mine[...] = (pair_acc[mine_at] + red0[...]).reshape(ncol, chunk, no)

    @pl.loop(1, ncol, unroll=5)
    def _(d):
        r1_copy(d).start()

    red1[col] = mine[col]

    lay_out(nch // 4, nch)
    sent_late(nset - 1)

    out_copy = pltpu.make_async_copy(out_bf16, fitted, out_sem)
    out_copy.start()

    @pl.loop(1, ncol)
    def _(d):
        r1_landed(lax.rem(col + d, ncol)).wait_recv()

    total = red1[0]
    for c in range(1, ncol):
        total = total + red1[c]
    red2[lax.div(row, 2)] = total
    for d in (2, 1, 3):
        r2_copy(d).start()
    for d in (1, 3, 2):
        r2_landed(d).wait_recv()

    total = red2[0]
    for z in range(1, nz):
        total = total + red2[z]
    red3[col] = total * F32(scale)

    @pl.loop(1, ncol, unroll=5)
    def _(d):
        r3_copy(d).start()

    @pl.loop(1, ncol, unroll=5)
    def _(d):
        r3_landed(lax.rem(col + d, ncol)).wait_recv()

    r4_copy = pltpu.make_async_remote_copy(
        src_ref=red3,
        dst_ref=red4,
        send_sem=r4_send,
        recv_sem=r4_recv,
        device_id=(sib, col),
        device_id_type=MESH,
    )
    r4_copy.start()
    pair[mine_at] = red3[...].reshape(mid, no)

    r0_copy.wait_send()

    @pl.loop(1, ncol)
    def _(d):
        r1_copy(d).wait_send()
        r3_copy(d).wait_send()

    for d in range(1, nz):
        r2_copy(d).wait_send()

    r4_copy.wait_recv()
    pair[theirs_at] = red4[...].reshape(mid, no)
    r4_copy.wait_send()
    out_copy.wait()


def on_device(ncol, nrow, integrals, occupancy, coeffs, metric):
    rows, nmu, basis = integrals.shape
    no = coeffs.shape[1]
    kq = NX * rows
    chunk = no // 2 // ncol
    scale = 1.0 / (rows * ncol * nmu * nrow)
    dims = (ncol, nrow, rows, nmu, basis, no, scale)
    lanes = no // 128
    dma = pltpu.SemaphoreType.DMA
    scratch = [
        pltpu.VMEM((NBUF, QC, nmu, basis), BF16),
        pltpu.VMEM((basis, no), BF16),
        pltpu.VMEM((rows // BLK, basis, no), BF16),
        pltpu.VMEM((lanes, QC * nmu, 128), F32),
        pltpu.VMEM((lanes, QC * nmu, 128), F32),
        pltpu.VMEM((NY, rows, kq), BF16),
        pltpu.VMEM((NX, rows, kq), BF16),
        pltpu.VMEM((nmu, NX, rows, no), BF16),
        pltpu.VMEM((nmu, rows, no), BF16),
        pltpu.VMEM((2, nmu, rows, no), BF16),
        pltpu.VMEM((nmu, rows, no), BF16),
        pltpu.VMEM((2, nmu, rows, no), BF16),
        pltpu.VMEM((lanes, rows * nmu, 128), F32),
        pltpu.VMEM((rows, nmu, no), BF16),
        pltpu.VMEM((2, 3, UNIT, 2 * rows, no), F32),
        pltpu.VMEM((no, no), F32),
        pltpu.VMEM((no // 2, no), F32),
        pltpu.VMEM((ncol, chunk, no), F32),
        pltpu.VMEM((ncol, chunk, no), F32),
        pltpu.VMEM((nrow // 2, chunk, no), F32),
        pltpu.VMEM((ncol, chunk, no), F32),
        pltpu.VMEM((ncol, chunk, no), F32),
        dma((NBUF,)),
        dma,
        dma,
        dma((NY - 1,)),
        dma((NY - 1,)),
        dma((NY - 1, nrow // 2 - 1)),
        dma((NY - 1, nrow // 2 - 1)),
        dma((NY - 1, nrow // 2)),
        dma((NY - 1, nrow // 2)),
        dma((2, 2, nmu // 2 // UNIT, 2)),
        dma((2, 2, nmu // 2 // UNIT, 2)),
        dma((2, 2, nmu // 2 // UNIT)),
        dma((2, 2, nmu // 2 // UNIT)),
        dma((2, 2, nmu // 2 // UNIT)),
        dma((2, 2, nmu // 2 // UNIT)),
        dma((2, nmu)),
        dma((2, nmu)),
        dma,
        dma,
        dma((ncol,)),
        dma((ncol,)),
        dma((nrow // 2,)),
        dma((nrow // 2,)),
        dma((ncol,)),
        dma((ncol,)),
        dma,
        dma,
        dma,
    ]
    anywhere = pl.BlockSpec(memory_space=pl.ANY)
    flops = 2 * rows * nmu * no * (basis + ncol * rows + no)
    return pl.pallas_call(
        functools.partial(kernel, dims),
        out_shape=(
            pltpu.VMEM((rows, nmu, no), BF16),
            pltpu.VMEM((no, no), F32),
        ),
        in_specs=[
            anywhere,
            pl.BlockSpec(memory_space=pltpu.SMEM),
            anywhere,
            anywhere,
        ],
        out_specs=(anywhere, pl.BlockSpec(memory_space=pltpu.VMEM)),
        scratch_shapes=scratch,
        compiler_params=pltpu.CompilerParams(
            collective_id=0, has_side_effects=True, vmem_limit_bytes=58 * 1024 * 1024
        ),
        cost_estimate=pl.CostEstimate(
            flops=flops, bytes_accessed=2 * rows * nmu * (basis + no), transcendentals=0
        ),
    )(integrals, occupancy.T, coeffs, metric)


def solution(mesh):
    placed = (P("col", "row", None), P(), P(), P("col", None))
    return jax.shard_map(
        functools.partial(on_device, mesh.shape["col"], mesh.shape["row"]),
        mesh=mesh,
        in_specs=placed,
        out_specs=(P("col", "row", None), P()),
        check_vma=False,
    )
```

```python
import functools

import jax
import jax.numpy as jnp
from jax import lax
from jax.experimental import pallas as pl
from jax.experimental.pallas import tpu as pltpu
from jax.sharding import PartitionSpec as P

BLK = 128
NX = 4
NY = 4
QC = 32
UNIT = 2
AHEAD = 2
LAG = 1
NBUF = 4
OPP, RIGHT, LEFT, OWN = range(4)
MESH = pl.DeviceIdType.MESH
F32 = jnp.float32
BF16 = jnp.bfloat16


def kernel(
    dims, integrals, occupancy, coeffs, metric, fitted, pair,
    ibuf, cbuf, cmask, stage_a, stage_b, mb, mbt, hbuf, opp_out, side_out, opp_in, side_in,
    rows_f32, out_bf16, pbuf, pair_acc, red0, mine, red1, red2, red3, red4,
    in_sem, c_sem, m_loc, m_send, m_recv, m2_send, m2_recv, m3_send, m3_recv,
    ag_send, ag_recv, fw_send, fw_recv, op_send, op_recv, sp_send, sp_recv, sd_send, sd_recv,
    r0_send, r0_recv, r1_send, r1_recv, r2_send, r2_recv, r3_send, r3_recv,
    r4_send, r4_recv, out_sem,
):
    ncol, nrow, rows, nmu, basis, no, scale = dims
    half = rows // 2
    kq = NX * rows
    per_set = nmu // 2
    nset = per_set // UNIT
    nz = nrow // 2
    row = lax.axis_index("row")
    sib = row + 1 - 2 * lax.rem(row, 2)
    col = lax.axis_index("col")
    x = lax.rem(col, NX)
    y = lax.div(col, NX)
    nab = rows // BLK
    nch = rows // QC

    def col_x(d):
        return y * NX + lax.rem(x + d, NX)

    def col_y(d):
        return lax.rem(y + d, NY) * NX + x

    ag_to = ((col_x(1), col_x(NX - 1)), (col_y(1), col_y(NY - 1)))
    rs_to = (ag_to[1], ag_to[0])
    at_x = tuple(lax.rem(x + d, NX) for d in (0, NX - 1, 1, 2))
    held = (at_x, (OWN, LEFT, RIGHT, OPP))

    def in_copy(ch):
        q = pl.ds(ch * QC, QC)
        slot = lax.rem(ch, NBUF)
        return pltpu.make_async_copy(integrals.at[q], ibuf.at[slot], in_sem.at[slot])

    c_copy = pltpu.make_async_copy(coeffs, cbuf, c_sem)
    c_copy.start()

    @pl.loop(0, NBUF)
    def _(ch):
        in_copy(ch).start()

    def m_own():
        src = metric.at[:, pl.ds(pl.multiple_of(y * kq, 128), kq)]
        return pltpu.make_async_copy(src, mb.at[OWN], m_loc)

    m_own().start()

    barrier = pltpu.get_barrier_semaphore()

    @pl.loop(1, ncol)
    def _(d):
        pl.semaphore_signal(
            barrier, inc=1, device_id=(row, lax.rem(col + d, ncol)), device_id_type=MESH
        )

    @pl.loop(1, nrow)
    def _(d):
        pl.semaphore_signal(
            barrier, inc=1, device_id=(lax.rem(row + d, nrow), col), device_id_type=MESH
        )

    slot_of = {1: RIGHT, 2: OPP, 3: LEFT}
    share = rows // nrow

    def rows_of(r):
        return pl.ds(pl.multiple_of(r * share, 16), share)

    def m_copy(d):
        yd = lax.rem(y + d, NY)
        return pltpu.make_async_remote_copy(
            src_ref=metric.at[rows_of(row), pl.ds(pl.multiple_of(yd * kq, 128), kq)],
            dst_ref=mb.at[slot_of[NY - d], rows_of(row)],
            send_sem=m_send.at[d - 1],
            recv_sem=m_recv.at[NY - d - 1],
            device_id=(row, col_y(d)),
            device_id_type=MESH,
        )

    def m_landed(s):
        return pltpu.make_async_remote_copy(
            src_ref=metric.at[rows_of(row), pl.ds(0, kq)],
            dst_ref=mb.at[slot_of[s], rows_of(row)],
            send_sem=m_send.at[s - 1],
            recv_sem=m_recv.at[s - 1],
            device_id=(row, col_y(s)),
            device_id_type=MESH,
        )

    def along_z(d):
        return lax.rem(row + 2 * d, nrow)

    def m_share(s, d):
        blk = mb.at[slot_of[s], rows_of(row)]
        return pltpu.make_async_remote_copy(
            src_ref=blk,
            dst_ref=blk,
            send_sem=m2_send.at[s - 1, d - 1],
            recv_sem=m2_recv.at[s - 1, nz - d - 1],
            device_id=(along_z(d), col),
            device_id_type=MESH,
        )

    def m_shared(s, d):
        blk = mb.at[slot_of[s], rows_of(along_z(d))]
        return pltpu.make_async_remote_copy(
            src_ref=blk,
            dst_ref=blk,
            send_sem=m2_send.at[s - 1, d - 1],
            recv_sem=m2_recv.at[s - 1, d - 1],
            device_id=(along_z(d), col),
            device_id_type=MESH,
        )

    def m_pass(s, d, mine=True):
        src = along_z(d) if mine else lax.rem(sib + 2 * d, nrow)
        blk = mb.at[slot_of[s], rows_of(src)]
        return pltpu.make_async_remote_copy(
            src_ref=blk,
            dst_ref=blk,
            send_sem=m3_send.at[s - 1, d],
            recv_sem=m3_recv.at[s - 1, d],
            device_id=(sib, col),
            device_id_type=MESH,
        )

    c_copy.wait()
    def make_mask(ab):
        @pl.loop(0, basis // BLK, unroll=4)
        def _(nb):
            on = jnp.full((BLK, no), occupancy[nb, col * nab + ab], jnp.int32) > 0
            at = pl.ds(pl.multiple_of(nb * BLK, BLK), BLK)
            kept = jnp.where(on, cbuf[at, :].astype(F32), 0.0)
            cmask[ab, at, :] = kept.astype(BF16)

    make_mask(0)

    pl.semaphore_wait(barrier, ncol + nrow - 2)

    for d in (2, 1, 3):
        m_copy(d).start()

    def transform(ch, ab, to):
        rowsin = ibuf[lax.rem(ch, NBUF)].reshape(QC * nmu, basis)
        res = jnp.dot(rowsin, cmask[ab], preferred_element_type=F32)
        for h in range(no // 128):
            to[h] = res[:, h * 128 : (h + 1) * 128]

    def relayout(ch, frm):
        q0 = pl.multiple_of(ch * QC, QC)
        for mu in range(nmu):
            own = held[mu // per_set][0]
            for h in range(no // 128):
                got = frm[h, pl.ds(mu, QC, stride=nmu), :]
                hbuf[mu, own, pl.ds(q0, QC), h * 128 : (h + 1) * 128] = got.astype(BF16)

    def mus(st, k):
        return pl.ds(st * per_set + k * UNIT, UNIT)

    def ag_copy(st, side, k, hf, blk=None, to=None):
        part_rows = pl.ds(hf * half, half)
        src = held[st][0] if blk is None else blk
        dst = (at_x[0], (LEFT, RIGHT)[side])[st] if to is None else to
        return pltpu.make_async_remote_copy(
            src_ref=hbuf.at[mus(st, k), src, part_rows],
            dst_ref=hbuf.at[mus(st, k), dst, part_rows],
            send_sem=ag_send.at[st, side, k, hf],
            recv_sem=ag_recv.at[st, side, k, hf],
            device_id=(row, ag_to[st][side]),
            device_id_type=MESH,
        )

    def ag_wait(st, side, k, hf):
        blk = held[st][1 + side]
        ag_copy(st, side, k, hf, blk, blk).wait_recv()

    def fw_copy(st, side, k, blk=None, to=None):
        part_rows = pl.ds(side * half, half)
        src = held[st][1 + side] if blk is None else blk
        dst = (at_x[1 + side], OPP)[st] if to is None else to
        return pltpu.make_async_remote_copy(
            src_ref=hbuf.at[mus(st, k), src, part_rows],
            dst_ref=hbuf.at[mus(st, k), dst, part_rows],
            send_sem=fw_send.at[st, side, k],
            recv_sem=fw_recv.at[st, side, k],
            device_id=(row, ag_to[st][side]),
            device_id_type=MESH,
        )

    def fw_wait(st, side, k):
        blk = held[st][3]
        fw_copy(st, side, k, blk, blk).wait_recv()

    def op_copy(st, side, k):
        part_rows = pl.ds(side * half, half)
        return pltpu.make_async_remote_copy(
            src_ref=opp_out.at[mus(st, k), part_rows],
            dst_ref=opp_in.at[mus(st, k), part_rows],
            send_sem=op_send.at[st, side, k],
            recv_sem=op_recv.at[st, side, k],
            device_id=(row, rs_to[st][side]),
            device_id_type=MESH,
        )

    def sp_copy(st, side, k):
        part_rows = pl.ds((1 - side) * half, half)
        return pltpu.make_async_remote_copy(
            src_ref=side_out.at[side, mus(st, k), part_rows],
            dst_ref=side_in.at[side, mus(st, k), part_rows],
            send_sem=sp_send.at[st, side, k],
            recv_sem=sp_recv.at[st, side, k],
            device_id=(row, rs_to[st][side]),
            device_id_type=MESH,
        )

    def sd_copy(st, side, mu):
        part_rows = pl.ds(side * half, half)
        return pltpu.make_async_remote_copy(
            src_ref=side_out.at[side, mu, part_rows],
            dst_ref=side_in.at[side, mu, part_rows],
            send_sem=sd_send.at[side, mu],
            recv_sem=sd_recv.at[side, mu],
            device_id=(row, rs_to[st][side]),
            device_id_type=MESH,
        )

    def ag_start(st, k):
        for step in range(2):
            ag_copy(st, 0, k, step).start()
            ag_copy(st, 1, k, 1 - step).start()

    def forward(st, k):
        for side in range(2):
            ag_wait(st, side, k, side)
            fw_copy(st, side, k).start()

    def product(st, k):
        block = (mb, mbt)[st]
        for side in range(2):
            ag_wait(st, side, k, 1 - side)
            fw_wait(st, side, k)

        @pl.loop(0, UNIT)
        def _(m):
            mu = st * per_set + k * UNIT + m
            full = hbuf[mu].reshape(kq, no)
            got = jnp.dot(block[...].reshape(NY * rows, kq), full, preferred_element_type=F32)
            opp_out[mu] = got[:rows].astype(BF16)
            for side in range(2):
                at = (1 + side) * rows
                first = got[at : at + half]
                second = got[at + half : at + rows]
                plain = pl.ds((1 - side) * half, half)
                side_out[side, mu, plain] = (second, first)[side].astype(BF16)
                pbuf[st, lax.rem(k, 3), m, pl.ds(side * half, half)] = (first, second)[side]
            pbuf[st, lax.rem(k, 3), m, pl.ds(rows, rows)] = got[3 * rows :]

        for side in range(2):
            op_copy(st, side, k).start()
        for side in range(2):
            sp_copy(st, side, k).start()

    def sides(k):
        for m in range(UNIT):
            for st in range(2):
                mu = st * per_set + k * UNIT + m
                for side in range(2):
                    if m == 0:
                        op_copy(st, side, k).wait_recv()
                    at = pl.ds(side * half, half)
                    side_out[side, mu, at] = (
                        pbuf[st, lax.rem(k, 3), m, at] + opp_in[mu, at].astype(F32)
                    ).astype(BF16)
                    sd_copy(st, side, mu).start()

    pair_acc[...] = jnp.zeros_like(pair_acc)

    def finish(k):
        for st in range(2):
            for side in range(2):
                sp_copy(st, side, k).wait_recv()

        @pl.loop(0, UNIT)
        def _(m):
            pairs = []
            for st in range(2):
                for side in range(2):
                    sd_copy(st, side, st * per_set + k * UNIT + m).wait_recv()
            for st in range(2):
                mu = st * per_set + k * UNIT + m
                own = pbuf[st, lax.rem(k, 3), m, pl.ds(rows, rows)]
                total = own + side_in[0, mu].astype(F32) + side_in[1, mu].astype(F32)
                done = total.astype(BF16)
                back = done.astype(F32)
                for h in range(no // 128):
                    at = pl.ds(mu, rows, stride=nmu)
                    rows_f32[h, at, :] = back[:, h * 128 : (h + 1) * 128]
                pairs.append(done)
            both = jnp.concatenate(pairs, axis=0)
            pair_acc[...] += lax.dot_general(
                both, both, (((0,), (0,)), ((), ())), preferred_element_type=F32
            )

    quarter = rows // 4

    def send_rows(begin, count):
        part_rows = pl.ds(pl.multiple_of(begin, QC), count)
        hf = lax.div(begin, half)
        for k in range(AHEAD):
            for st in range(2):
                for side in range(2):
                    pltpu.make_async_remote_copy(
                        src_ref=hbuf.at[mus(st, k), held[st][0], part_rows],
                        dst_ref=hbuf.at[
                            mus(st, k), (at_x[0], (LEFT, RIGHT)[side])[st], part_rows
                        ],
                        send_sem=ag_send.at[st, side, k, hf],
                        recv_sem=ag_recv.at[st, side, k, hf],
                        device_id=(row, ag_to[st][side]),
                        device_id_type=MESH,
                    ).start()

    stage_b[...] = jnp.zeros_like(stage_b)

    @pl.loop(0, nch // 2)
    def _(j):
        ch = 2 * j
        ab = lax.div(ch * QC, BLK)

        for later in range(1, nab):

            @pl.when(ch == later * (nch // nab))
            def _():
                make_mask(later)

        in_copy(ch).wait()
        in_copy(ch + 1).wait()
        transform(ch, ab, stage_a)
        relayout(lax.max(ch - 1, 0), stage_b)

        @pl.when(j == 1)
        def _():
            send_rows(QC, quarter - QC)

        @pl.when(j >= 2)
        def _():
            send_rows((j - 1) * quarter, quarter)

        @pl.when(j == 1)
        def _():
            for s in (2, 1, 3):
                m_landed(s).wait_recv()
                for d in (2, 1, 3):
                    m_share(s, d).start()
                m_pass(s, 0).start()

        transform(ch + 1, ab, stage_b)
        relayout(ch, stage_a)

        @pl.when(j == 0)
        def _():
            send_rows(0, QC)

        @pl.when(ch + NBUF < nch)
        def _():
            in_copy(ch + NBUF).start()
            in_copy(ch + NBUF + 1).start()

    relayout(nch - 1, stage_b)
    send_rows((nch // 2 - 1) * quarter, quarter)

    def metric_sent():
        for s in range(1, NY):
            m_copy(s).wait_send()
            for d in range(nz):
                m_pass(s, d).wait_send()
            for d in range(1, nz):
                m_share(s, d).wait_send()

    def sent_early(k):
        for st in range(2):
            for side in range(2):
                for hf in range(2):
                    ag_copy(st, side, k, hf).wait_send()
                fw_copy(st, side, k).wait_send()
                op_copy(st, side, k).wait_send()

    def sent_late(k):
        for st in range(2):
            for side in range(2):
                sp_copy(st, side, k).wait_send()
                for m in range(UNIT):
                    sd_copy(st, side, st * per_set + k * UNIT + m).wait_send()

    def metric_ready():
        m_own().wait()
        for d in range(nz):
            for s in (2, 1, 3):
                m_pass(s, d, False).wait_recv()

    def transpose_metric():
        offs = {OPP: 2, RIGHT: 1, LEFT: NX - 1, OWN: 0}
        for to, d in offs.items():
            at = pl.ds(pl.multiple_of(lax.rem(x + d, NX) * rows, 128), rows)

            @pl.loop(0, NY)
            def _(s):
                mbt[to, :, pl.ds(pl.multiple_of(s * rows, 128), rows)] = mb[s, :, at].T

    @pl.loop(0, nset + LAG + 2)
    def _(k):
        @pl.when(k + AHEAD < nset)
        def _():
            ag_start(0, k + AHEAD)
            ag_start(1, k + AHEAD)

        @pl.when(k < nset)
        def _():
            forward(0, k)
            forward(1, k)

        @pl.when(k == 0)
        def _():
            for s in (2, 1, 3):
                for d in (1, 3, 2):
                    m_shared(s, d).wait_recv()
                    m_pass(s, d).start()

        @pl.when((k >= LAG) & (k < nset + LAG))
        def _():
            @pl.when(k == LAG)
            def _():
                metric_ready()

            product(0, k - LAG)

            @pl.when(k == LAG)
            def _():
                transpose_metric()

            product(1, k - LAG)

        @pl.when((k >= LAG + 1) & (k < nset + LAG + 1))
        def _():
            sides(k - LAG - 1)
            sent_early(k - LAG - 1)

        @pl.when(k == LAG + 1)
        def _():
            metric_sent()

        @pl.when(k >= LAG + 2)
        def _():
            finish(k - LAG - 2)

        @pl.when((k >= LAG + 2) & (k < nset + LAG + 1))
        def _():
            sent_late(k - LAG - 2)

    chunk = no // 2 // ncol
    core = lax.rem(row, 2)
    mid = no // 2
    mine_at = pl.ds(pl.multiple_of(core * mid, 8), mid)
    theirs_at = pl.ds(pl.multiple_of((1 - core) * mid, 8), mid)

    r0_copy = pltpu.make_async_remote_copy(
        src_ref=pair_acc.at[theirs_at],
        dst_ref=red0,
        send_sem=r0_send,
        recv_sem=r0_recv,
        device_id=(sib, col),
        device_id_type=MESH,
    )
    r0_copy.start()

    def r1_copy(d):
        to = lax.rem(col + d, ncol)
        return pltpu.make_async_remote_copy(
            src_ref=mine.at[to],
            dst_ref=red1.at[col],
            send_sem=r1_send.at[d],
            recv_sem=r1_recv.at[col],
            device_id=(row, to),
            device_id_type=MESH,
        )

    def r1_landed(src):
        return pltpu.make_async_remote_copy(
            src_ref=mine.at[src],
            dst_ref=red1.at[src],
            send_sem=r1_send.at[0],
            recv_sem=r1_recv.at[src],
            device_id=(row, src),
            device_id_type=MESH,
        )

    def r2_copy(d):
        z = lax.div(row, 2)
        return pltpu.make_async_remote_copy(
            src_ref=red2.at[z],
            dst_ref=red2.at[z],
            send_sem=r2_send.at[d],
            recv_sem=r2_recv.at[z],
            device_id=(along_z(d), col),
            device_id_type=MESH,
        )

    def r2_landed(d):
        z = lax.div(along_z(d), 2)
        return pltpu.make_async_remote_copy(
            src_ref=red2.at[z],
            dst_ref=red2.at[z],
            send_sem=r2_send.at[d],
            recv_sem=r2_recv.at[z],
            device_id=(along_z(d), col),
            device_id_type=MESH,
        )

    def r3_copy(d):
        to = lax.rem(col + d, ncol)
        return pltpu.make_async_remote_copy(
            src_ref=red3.at[col],
            dst_ref=red3.at[col],
            send_sem=r3_send.at[d],
            recv_sem=r3_recv.at[col],
            device_id=(row, to),
            device_id_type=MESH,
        )

    def r3_landed(src):
        return pltpu.make_async_remote_copy(
            src_ref=red3.at[src],
            dst_ref=red3.at[src],
            send_sem=r3_send.at[0],
            recv_sem=r3_recv.at[src],
            device_id=(row, src),
            device_id_type=MESH,
        )

    def lay_out(begin, end):
        @pl.loop(begin, end)
        def _(ch):
            at = pl.ds(pl.multiple_of(ch * QC * nmu, QC), QC * nmu)
            for h in range(no // 128):
                out_bf16[pl.ds(ch * QC, QC), :, h * 128 : (h + 1) * 128] = (
                    rows_f32[h, at, :].astype(BF16).reshape(QC, nmu, 128)
                )

    lay_out(0, nch // 4)
    r0_copy.wait_recv()
    mine[...] = (pair_acc[mine_at] + red0[...]).reshape(ncol, chunk, no)

    @pl.loop(1, ncol, unroll=5)
    def _(d):
        r1_copy(d).start()

    red1[col] = mine[col]

    lay_out(nch // 4, nch)
    sent_late(nset - 1)

    out_copy = pltpu.make_async_copy(out_bf16, fitted, out_sem)
    out_copy.start()

    @pl.loop(1, ncol)
    def _(d):
        r1_landed(lax.rem(col + d, ncol)).wait_recv()

    total = red1[0]
    for c in range(1, ncol):
        total = total + red1[c]
    red2[lax.div(row, 2)] = total
    for d in (2, 1, 3):
        r2_copy(d).start()
    for d in (1, 3, 2):
        r2_landed(d).wait_recv()

    total = red2[0]
    for z in range(1, nz):
        total = total + red2[z]
    red3[col] = total * F32(scale)

    @pl.loop(1, ncol, unroll=5)
    def _(d):
        r3_copy(d).start()

    @pl.loop(1, ncol, unroll=5)
    def _(d):
        r3_landed(lax.rem(col + d, ncol)).wait_recv()

    r4_copy = pltpu.make_async_remote_copy(
        src_ref=red3,
        dst_ref=red4,
        send_sem=r4_send,
        recv_sem=r4_recv,
        device_id=(sib, col),
        device_id_type=MESH,
    )
    r4_copy.start()
    pair[mine_at] = red3[...].reshape(mid, no)

    r0_copy.wait_send()

    @pl.loop(1, ncol)
    def _(d):
        r1_copy(d).wait_send()
        r3_copy(d).wait_send()

    for d in range(1, nz):
        r2_copy(d).wait_send()

    r4_copy.wait_recv()
    pair[theirs_at] = red4[...].reshape(mid, no)
    r4_copy.wait_send()
    out_copy.wait()


def on_device(ncol, nrow, integrals, occupancy, coeffs, metric):
    rows, nmu, basis = integrals.shape
    no = coeffs.shape[1]
    kq = NX * rows
    chunk = no // 2 // ncol
    scale = 1.0 / (rows * ncol * nmu * nrow)
    dims = (ncol, nrow, rows, nmu, basis, no, scale)
    lanes = no // 128
    dma = pltpu.SemaphoreType.DMA
    scratch = [
        pltpu.VMEM((NBUF, QC, nmu, basis), BF16),
        pltpu.VMEM((basis, no), BF16),
        pltpu.VMEM((rows // BLK, basis, no), BF16),
        pltpu.VMEM((lanes, QC * nmu, 128), F32),
        pltpu.VMEM((lanes, QC * nmu, 128), F32),
        pltpu.VMEM((NY, rows, kq), BF16),
        pltpu.VMEM((NX, rows, kq), BF16),
        pltpu.VMEM((nmu, NX, rows, no), BF16),
        pltpu.VMEM((nmu, rows, no), BF16),
        pltpu.VMEM((2, nmu, rows, no), BF16),
        pltpu.VMEM((nmu, rows, no), BF16),
        pltpu.VMEM((2, nmu, rows, no), BF16),
        pltpu.VMEM((lanes, rows * nmu, 128), F32),
        pltpu.VMEM((rows, nmu, no), BF16),
        pltpu.VMEM((2, 3, UNIT, 2 * rows, no), F32),
        pltpu.VMEM((no, no), F32),
        pltpu.VMEM((no // 2, no), F32),
        pltpu.VMEM((ncol, chunk, no), F32),
        pltpu.VMEM((ncol, chunk, no), F32),
        pltpu.VMEM((nrow // 2, chunk, no), F32),
        pltpu.VMEM((ncol, chunk, no), F32),
        pltpu.VMEM((ncol, chunk, no), F32),
        dma((NBUF,)),
        dma,
        dma,
        dma((NY - 1,)),
        dma((NY - 1,)),
        dma((NY - 1, nrow // 2 - 1)),
        dma((NY - 1, nrow // 2 - 1)),
        dma((NY - 1, nrow // 2)),
        dma((NY - 1, nrow // 2)),
        dma((2, 2, nmu // 2 // UNIT, 2)),
        dma((2, 2, nmu // 2 // UNIT, 2)),
        dma((2, 2, nmu // 2 // UNIT)),
        dma((2, 2, nmu // 2 // UNIT)),
        dma((2, 2, nmu // 2 // UNIT)),
        dma((2, 2, nmu // 2 // UNIT)),
        dma((2, 2, nmu // 2 // UNIT)),
        dma((2, 2, nmu // 2 // UNIT)),
        dma((2, nmu)),
        dma((2, nmu)),
        dma,
        dma,
        dma((ncol,)),
        dma((ncol,)),
        dma((nrow // 2,)),
        dma((nrow // 2,)),
        dma((ncol,)),
        dma((ncol,)),
        dma,
        dma,
        dma,
    ]
    anywhere = pl.BlockSpec(memory_space=pl.ANY)
    flops = 2 * rows * nmu * no * (basis + ncol * rows + no)
    return pl.pallas_call(
        functools.partial(kernel, dims),
        out_shape=(
            pltpu.VMEM((rows, nmu, no), BF16),
            pltpu.VMEM((no, no), F32),
        ),
        in_specs=[
            anywhere,
            pl.BlockSpec(memory_space=pltpu.SMEM),
            anywhere,
            anywhere,
        ],
        out_specs=(anywhere, pl.BlockSpec(memory_space=pltpu.VMEM)),
        scratch_shapes=scratch,
        compiler_params=pltpu.CompilerParams(
            collective_id=0, has_side_effects=True, vmem_limit_bytes=58 * 1024 * 1024
        ),
        cost_estimate=pl.CostEstimate(
            flops=flops, bytes_accessed=2 * rows * nmu * (basis + no), transcendentals=0
        ),
    )(integrals, occupancy.T, coeffs, metric)


def solution(mesh):
    placed = (P("col", "row", None), P(), P(), P("col", None))
    return jax.shard_map(
        functools.partial(on_device, mesh.shape["col"], mesh.shape["row"]),
        mesh=mesh,
        in_specs=placed,
        out_specs=(P("col", "row", None), P()),
        check_vma=False,
    )
```

```python
import functools

import jax
import jax.numpy as jnp
from jax import lax
from jax.experimental import pallas as pl
from jax.experimental.pallas import tpu as pltpu
from jax.sharding import PartitionSpec as P

BLK = 128
NX = 4
NY = 4
QC = 32
UNIT = 1
AHEAD = 4
LAG = 2
SIDES = LAG + 2
FINISH = SIDES + 2
RING = FINISH - LAG + 1
NBUF = 4
OPP, RIGHT, LEFT, OWN = range(4)
MESH = pl.DeviceIdType.MESH
F32 = jnp.float32
BF16 = jnp.bfloat16


def kernel(
    dims, integrals, occupancy, coeffs, metric, fitted, pair,
    ibuf, cbuf, cmask, stage_a, stage_b, mb, mbt, hbuf, opp_out, side_out, opp_in, side_in,
    rows_f32, out_bf16, pbuf, pair_acc, red0, mine, red1, red2, red3, red4,
    in_sem, c_sem, m_loc, m_send, m_recv, m2_send, m2_recv, m3_send, m3_recv,
    ag_send, ag_recv, fw_send, fw_recv, op_send, op_recv, sd_send, sd_recv,
    r0_send, r0_recv, r1_send, r1_recv, r2_send, r2_recv, r3_send, r3_recv,
    r4_send, r4_recv, out_sem,
):
    ncol, nrow, rows, nmu, basis, no, scale = dims
    half = rows // 2
    kq = NX * rows
    per_set = nmu // 2
    nset = per_set // UNIT
    nz = nrow // 2
    row = lax.axis_index("row")
    sib = row + 1 - 2 * lax.rem(row, 2)
    col = lax.axis_index("col")
    x = lax.rem(col, NX)
    y = lax.div(col, NX)
    nab = rows // BLK
    nch = rows // QC

    def col_x(d):
        return y * NX + lax.rem(x + d, NX)

    def col_y(d):
        return lax.rem(y + d, NY) * NX + x

    ag_to = ((col_x(1), col_x(NX - 1)), (col_y(1), col_y(NY - 1)))
    rs_to = (ag_to[1], ag_to[0])
    at_x = tuple(lax.rem(x + d, NX) for d in (0, NX - 1, 1, 2))
    held = (at_x, (OWN, LEFT, RIGHT, OPP))

    def in_copy(ch):
        q = pl.ds(ch * QC, QC)
        slot = lax.rem(ch, NBUF)
        return pltpu.make_async_copy(integrals.at[q], ibuf.at[slot], in_sem.at[slot])

    c_copy = pltpu.make_async_copy(coeffs, cbuf, c_sem)
    c_copy.start()

    @pl.loop(0, NBUF)
    def _(ch):
        in_copy(ch).start()

    def m_own():
        src = metric.at[:, pl.ds(pl.multiple_of(y * kq, 128), kq)]
        return pltpu.make_async_copy(src, mb.at[OWN], m_loc)

    m_own().start()

    barrier = pltpu.get_barrier_semaphore()

    @pl.loop(1, ncol)
    def _(d):
        pl.semaphore_signal(
            barrier, inc=1, device_id=(row, lax.rem(col + d, ncol)), device_id_type=MESH
        )

    @pl.loop(1, nrow)
    def _(d):
        pl.semaphore_signal(
            barrier, inc=1, device_id=(lax.rem(row + d, nrow), col), device_id_type=MESH
        )

    slot_of = {1: RIGHT, 2: OPP, 3: LEFT}
    share = rows // nrow

    def rows_of(r):
        return pl.ds(pl.multiple_of(r * share, 16), share)

    def m_copy(d):
        yd = lax.rem(y + d, NY)
        return pltpu.make_async_remote_copy(
            src_ref=metric.at[rows_of(row), pl.ds(pl.multiple_of(yd * kq, 128), kq)],
            dst_ref=mb.at[slot_of[NY - d], rows_of(row)],
            send_sem=m_send.at[d - 1],
            recv_sem=m_recv.at[NY - d - 1],
            device_id=(row, col_y(d)),
            device_id_type=MESH,
        )

    def m_landed(s):
        return pltpu.make_async_remote_copy(
            src_ref=metric.at[rows_of(row), pl.ds(0, kq)],
            dst_ref=mb.at[slot_of[s], rows_of(row)],
            send_sem=m_send.at[s - 1],
            recv_sem=m_recv.at[s - 1],
            device_id=(row, col_y(s)),
            device_id_type=MESH,
        )

    def along_z(d):
        return lax.rem(row + 2 * d, nrow)

    def m_share(s, d):
        blk = mb.at[slot_of[s], rows_of(row)]
        return pltpu.make_async_remote_copy(
            src_ref=blk,
            dst_ref=blk,
            send_sem=m2_send.at[s - 1, d - 1],
            recv_sem=m2_recv.at[s - 1, nz - d - 1],
            device_id=(along_z(d), col),
            device_id_type=MESH,
        )

    def m_shared(s, d):
        blk = mb.at[slot_of[s], rows_of(along_z(d))]
        return pltpu.make_async_remote_copy(
            src_ref=blk,
            dst_ref=blk,
            send_sem=m2_send.at[s - 1, d - 1],
            recv_sem=m2_recv.at[s - 1, d - 1],
            device_id=(along_z(d), col),
            device_id_type=MESH,
        )

    def m_pass(s, d, mine=True):
        src = along_z(d) if mine else lax.rem(sib + 2 * d, nrow)
        blk = mb.at[slot_of[s], rows_of(src)]
        return pltpu.make_async_remote_copy(
            src_ref=blk,
            dst_ref=blk,
            send_sem=m3_send.at[s - 1, d],
            recv_sem=m3_recv.at[s - 1, d],
            device_id=(sib, col),
            device_id_type=MESH,
        )

    c_copy.wait()
    for ab in range(nab):

        @pl.loop(0, basis // BLK, unroll=4)
        def _(nb):
            on = jnp.full((BLK, no), occupancy[nb, col * nab + ab], jnp.int32) > 0
            at = pl.ds(pl.multiple_of(nb * BLK, BLK), BLK)
            kept = jnp.where(on, cbuf[at, :].astype(F32), 0.0)
            cmask[ab, at, :] = kept.astype(BF16)

    pl.semaphore_wait(barrier, ncol + nrow - 2)

    for d in (2, 1, 3):
        m_copy(d).start()

    def transform(ch, ab, to):
        rowsin = ibuf[lax.rem(ch, NBUF)].reshape(QC * nmu, basis)
        res = jnp.dot(rowsin, cmask[ab], preferred_element_type=F32)
        for h in range(no // 128):
            to[h] = res[:, h * 128 : (h + 1) * 128]

    def relayout(ch, frm):
        q0 = pl.multiple_of(ch * QC, QC)
        for mu in range(nmu):
            own = held[mu // per_set][0]
            for h in range(no // 128):
                got = frm[h, pl.ds(mu, QC, stride=nmu), :]
                hbuf[mu, own, pl.ds(q0, QC), h * 128 : (h + 1) * 128] = got.astype(BF16)

    def mus(st, k):
        return pl.ds(st * per_set + k * UNIT, UNIT)

    def ag_copy(st, side, k, hf, blk=None, to=None):
        part_rows = pl.ds(hf * half, half)
        src = held[st][0] if blk is None else blk
        dst = (at_x[0], (LEFT, RIGHT)[side])[st] if to is None else to
        return pltpu.make_async_remote_copy(
            src_ref=hbuf.at[mus(st, k), src, part_rows],
            dst_ref=hbuf.at[mus(st, k), dst, part_rows],
            send_sem=ag_send.at[st, side, k, hf],
            recv_sem=ag_recv.at[st, side, k, hf],
            device_id=(row, ag_to[st][side]),
            device_id_type=MESH,
        )

    def ag_wait(st, side, k, hf):
        blk = held[st][1 + side]
        ag_copy(st, side, k, hf, blk, blk).wait_recv()

    def fw_copy(st, side, k, blk=None, to=None):
        part_rows = pl.ds(side * half, half)
        src = held[st][1 + side] if blk is None else blk
        dst = (at_x[1 + side], OPP)[st] if to is None else to
        return pltpu.make_async_remote_copy(
            src_ref=hbuf.at[mus(st, k), src, part_rows],
            dst_ref=hbuf.at[mus(st, k), dst, part_rows],
            send_sem=fw_send.at[st, side, k],
            recv_sem=fw_recv.at[st, side, k],
            device_id=(row, ag_to[st][side]),
            device_id_type=MESH,
        )

    def fw_wait(st, side, k):
        blk = held[st][3]
        fw_copy(st, side, k, blk, blk).wait_recv()

    def op_copy(st, side, k):
        part_rows = pl.ds(side * half, half)
        return pltpu.make_async_remote_copy(
            src_ref=opp_out.at[mus(st, k), part_rows],
            dst_ref=opp_in.at[mus(st, k), part_rows],
            send_sem=op_send.at[st, side, k],
            recv_sem=op_recv.at[st, side, k],
            device_id=(row, rs_to[st][side]),
            device_id_type=MESH,
        )

    def sd_copy(st, side, mu):
        return pltpu.make_async_remote_copy(
            src_ref=side_out.at[side, mu],
            dst_ref=side_in.at[side, mu],
            send_sem=sd_send.at[side, mu],
            recv_sem=sd_recv.at[side, mu],
            device_id=(row, rs_to[st][side]),
            device_id_type=MESH,
        )

    def ag_start(st, k):
        for step in range(2):
            ag_copy(st, 0, k, step).start()
            ag_copy(st, 1, k, 1 - step).start()

    def forward(st, k):
        for side in range(2):
            ag_wait(st, side, k, side)
            fw_copy(st, side, k).start()

    def product(st, k):
        block = (mb, mbt)[st]
        for side in range(2):
            ag_wait(st, side, k, 1 - side)
            fw_wait(st, side, k)

        @pl.loop(0, UNIT)
        def _(m):
            mu = st * per_set + k * UNIT + m
            full = hbuf[mu].reshape(kq, no)
            got = jnp.dot(block[...].reshape(NY * rows, kq), full, preferred_element_type=F32)
            opp_out[mu] = got[:rows].astype(BF16)
            for side in range(2):
                at = (1 + side) * rows
                first = got[at : at + half]
                second = got[at + half : at + rows]
                plain = pl.ds((1 - side) * half, half)
                side_out[side, mu, plain] = (second, first)[side].astype(BF16)
                pbuf[st, lax.rem(k, RING), m, pl.ds(side * half, half)] = (first, second)[side]
            pbuf[st, lax.rem(k, RING), m, pl.ds(rows, rows)] = got[3 * rows :]

        op_copy(st, 0, k).start()
        op_copy(st, 1, k).start()

    def sides(k):
        for m in range(UNIT):
            for st in range(2):
                mu = st * per_set + k * UNIT + m
                for side in range(2):
                    if m == 0:
                        op_copy(st, side, k).wait_recv()
                    at = pl.ds(side * half, half)
                    side_out[side, mu, at] = (
                        pbuf[st, lax.rem(k, RING), m, at] + opp_in[mu, at].astype(F32)
                    ).astype(BF16)
                    sd_copy(st, side, mu).start()

    pair_acc[...] = jnp.zeros_like(pair_acc)

    def finish(k):
        @pl.loop(0, UNIT)
        def _(m):
            pairs = []
            for st in range(2):
                for side in range(2):
                    sd_copy(st, side, st * per_set + k * UNIT + m).wait_recv()
            for st in range(2):
                mu = st * per_set + k * UNIT + m
                own = pbuf[st, lax.rem(k, RING), m, pl.ds(rows, rows)]
                total = own + side_in[0, mu].astype(F32) + side_in[1, mu].astype(F32)
                done = total.astype(BF16)
                back = done.astype(F32)
                for h in range(no // 128):
                    at = pl.ds(mu, rows, stride=nmu)
                    rows_f32[h, at, :] = back[:, h * 128 : (h + 1) * 128]
                pairs.append(done)
            both = jnp.concatenate(pairs, axis=0)
            pair_acc[...] += lax.dot_general(
                both, both, (((0,), (0,)), ((), ())), preferred_element_type=F32
            )

    quarter = rows // 4

    def send_quarter(qt):
        part_rows = pl.ds(pl.multiple_of(qt * quarter, quarter), quarter)
        for k in range(AHEAD):
            for st in range(2):
                for side in range(2):
                    pltpu.make_async_remote_copy(
                        src_ref=hbuf.at[mus(st, k), held[st][0], part_rows],
                        dst_ref=hbuf.at[
                            mus(st, k), (at_x[0], (LEFT, RIGHT)[side])[st], part_rows
                        ],
                        send_sem=ag_send.at[st, side, k, lax.div(qt, 2)],
                        recv_sem=ag_recv.at[st, side, k, lax.div(qt, 2)],
                        device_id=(row, ag_to[st][side]),
                        device_id_type=MESH,
                    ).start()

    stage_b[...] = jnp.zeros_like(stage_b)

    @pl.loop(0, nch // 2)
    def _(j):
        ch = 2 * j
        ab = lax.div(ch * QC, BLK)
        in_copy(ch).wait()
        in_copy(ch + 1).wait()
        transform(ch, ab, stage_a)
        relayout(lax.max(ch - 1, 0), stage_b)

        @pl.when(j >= 1)
        def _():
            send_quarter(j - 1)

        @pl.when(j == 1)
        def _():
            for s in (2, 1, 3):
                m_landed(s).wait_recv()
                for d in (2, 1, 3):
                    m_share(s, d).start()
                m_pass(s, 0).start()

        transform(ch + 1, ab, stage_b)
        relayout(ch, stage_a)

        @pl.when(ch + NBUF < nch)
        def _():
            in_copy(ch + NBUF).start()
            in_copy(ch + NBUF + 1).start()

    relayout(nch - 1, stage_b)
    send_quarter(nch // 2 - 1)

    def metric_sent():
        for s in range(1, NY):
            m_copy(s).wait_send()
            for d in range(nz):
                m_pass(s, d).wait_send()
            for d in range(1, nz):
                m_share(s, d).wait_send()

    def sent_early(k):
        for st in range(2):
            for side in range(2):
                for hf in range(2):
                    ag_copy(st, side, k, hf).wait_send()
                fw_copy(st, side, k).wait_send()
                op_copy(st, side, k).wait_send()

    def sent_late(k):
        for st in range(2):
            for side in range(2):
                for m in range(UNIT):
                    sd_copy(st, side, st * per_set + k * UNIT + m).wait_send()

    def metric_ready():
        m_own().wait()
        for d in range(nz):
            for s in (2, 1, 3):
                m_pass(s, d, False).wait_recv()

    def transpose_metric():
        offs = {OPP: 2, RIGHT: 1, LEFT: NX - 1, OWN: 0}
        for to, d in offs.items():
            at = pl.ds(pl.multiple_of(lax.rem(x + d, NX) * rows, 128), rows)

            @pl.loop(0, NY)
            def _(s):
                mbt[to, :, pl.ds(pl.multiple_of(s * rows, 128), rows)] = mb[s, :, at].T

    @pl.loop(0, nset + FINISH)
    def _(k):
        @pl.when(k + AHEAD < nset)
        def _():
            ag_start(0, k + AHEAD)
            ag_start(1, k + AHEAD)

        @pl.when(k < nset)
        def _():
            forward(0, k)
            forward(1, k)

        @pl.when(k == LAG - 1)
        def _():
            for s in (2, 1, 3):
                for d in (1, 3, 2):
                    m_shared(s, d).wait_recv()
                    m_pass(s, d).start()

        @pl.when((k >= LAG) & (k < nset + LAG))
        def _():
            @pl.when(k == LAG)
            def _():
                metric_ready()

            product(0, k - LAG)

            @pl.when(k == LAG)
            def _():
                transpose_metric()

            product(1, k - LAG)

        @pl.when((k >= SIDES) & (k < nset + SIDES))
        def _():
            sides(k - SIDES)
            sent_early(k - SIDES)

        @pl.when(k == SIDES)
        def _():
            metric_sent()

        @pl.when(k >= FINISH)
        def _():
            finish(k - FINISH)

        @pl.when((k >= FINISH) & (k < nset + FINISH - 1))
        def _():
            sent_late(k - FINISH)

    chunk = no // 2 // ncol
    core = lax.rem(row, 2)
    mid = no // 2
    mine_at = pl.ds(pl.multiple_of(core * mid, 8), mid)
    theirs_at = pl.ds(pl.multiple_of((1 - core) * mid, 8), mid)

    r0_copy = pltpu.make_async_remote_copy(
        src_ref=pair_acc.at[theirs_at],
        dst_ref=red0,
        send_sem=r0_send,
        recv_sem=r0_recv,
        device_id=(sib, col),
        device_id_type=MESH,
    )
    r0_copy.start()

    def r1_copy(d):
        to = lax.rem(col + d, ncol)
        return pltpu.make_async_remote_copy(
            src_ref=mine.at[to],
            dst_ref=red1.at[col],
            send_sem=r1_send.at[d],
            recv_sem=r1_recv.at[col],
            device_id=(row, to),
            device_id_type=MESH,
        )

    def r1_landed(src):
        return pltpu.make_async_remote_copy(
            src_ref=mine.at[src],
            dst_ref=red1.at[src],
            send_sem=r1_send.at[0],
            recv_sem=r1_recv.at[src],
            device_id=(row, src),
            device_id_type=MESH,
        )

    def r2_copy(d):
        z = lax.div(row, 2)
        return pltpu.make_async_remote_copy(
            src_ref=red2.at[z],
            dst_ref=red2.at[z],
            send_sem=r2_send.at[d],
            recv_sem=r2_recv.at[z],
            device_id=(along_z(d), col),
            device_id_type=MESH,
        )

    def r2_landed(d):
        z = lax.div(along_z(d), 2)
        return pltpu.make_async_remote_copy(
            src_ref=red2.at[z],
            dst_ref=red2.at[z],
            send_sem=r2_send.at[d],
            recv_sem=r2_recv.at[z],
            device_id=(along_z(d), col),
            device_id_type=MESH,
        )

    def r3_copy(d):
        to = lax.rem(col + d, ncol)
        return pltpu.make_async_remote_copy(
            src_ref=red3.at[col],
            dst_ref=red3.at[col],
            send_sem=r3_send.at[d],
            recv_sem=r3_recv.at[col],
            device_id=(row, to),
            device_id_type=MESH,
        )

    def r3_landed(src):
        return pltpu.make_async_remote_copy(
            src_ref=red3.at[src],
            dst_ref=red3.at[src],
            send_sem=r3_send.at[0],
            recv_sem=r3_recv.at[src],
            device_id=(row, src),
            device_id_type=MESH,
        )

    def lay_out(begin, end):
        @pl.loop(begin, end)
        def _(ch):
            at = pl.ds(pl.multiple_of(ch * QC * nmu, QC), QC * nmu)
            for h in range(no // 128):
                out_bf16[pl.ds(ch * QC, QC), :, h * 128 : (h + 1) * 128] = (
                    rows_f32[h, at, :].astype(BF16).reshape(QC, nmu, 128)
                )

    lay_out(0, nch // 4)
    r0_copy.wait_recv()
    mine[...] = (pair_acc[mine_at] + red0[...]).reshape(ncol, chunk, no)

    @pl.loop(1, ncol, unroll=5)
    def _(d):
        r1_copy(d).start()

    red1[col] = mine[col]

    lay_out(nch // 4, nch)
    sent_late(nset - 1)

    out_copy = pltpu.make_async_copy(out_bf16, fitted, out_sem)
    out_copy.start()

    @pl.loop(1, ncol)
    def _(d):
        r1_landed(lax.rem(col + d, ncol)).wait_recv()

    total = red1[0]
    for c in range(1, ncol):
        total = total + red1[c]
    red2[lax.div(row, 2)] = total
    for d in (2, 1, 3):
        r2_copy(d).start()
    for d in (1, 3, 2):
        r2_landed(d).wait_recv()

    total = red2[0]
    for z in range(1, nz):
        total = total + red2[z]
    red3[col] = total * F32(scale)

    @pl.loop(1, ncol, unroll=5)
    def _(d):
        r3_copy(d).start()

    @pl.loop(1, ncol, unroll=5)
    def _(d):
        r3_landed(lax.rem(col + d, ncol)).wait_recv()

    r4_copy = pltpu.make_async_remote_copy(
        src_ref=red3,
        dst_ref=red4,
        send_sem=r4_send,
        recv_sem=r4_recv,
        device_id=(sib, col),
        device_id_type=MESH,
    )
    r4_copy.start()
    pair[mine_at] = red3[...].reshape(mid, no)

    r0_copy.wait_send()

    @pl.loop(1, ncol)
    def _(d):
        r1_copy(d).wait_send()
        r3_copy(d).wait_send()

    for d in range(1, nz):
        r2_copy(d).wait_send()

    r4_copy.wait_recv()
    pair[theirs_at] = red4[...].reshape(mid, no)
    r4_copy.wait_send()
    out_copy.wait()


def on_device(ncol, nrow, integrals, occupancy, coeffs, metric):
    rows, nmu, basis = integrals.shape
    no = coeffs.shape[1]
    kq = NX * rows
    chunk = no // 2 // ncol
    scale = 1.0 / (rows * ncol * nmu * nrow)
    dims = (ncol, nrow, rows, nmu, basis, no, scale)
    lanes = no // 128
    dma = pltpu.SemaphoreType.DMA
    scratch = [
        pltpu.VMEM((NBUF, QC, nmu, basis), BF16),
        pltpu.VMEM((basis, no), BF16),
        pltpu.VMEM((rows // BLK, basis, no), BF16),
        pltpu.VMEM((lanes, QC * nmu, 128), F32),
        pltpu.VMEM((lanes, QC * nmu, 128), F32),
        pltpu.VMEM((NY, rows, kq), BF16),
        pltpu.VMEM((NX, rows, kq), BF16),
        pltpu.VMEM((nmu, NX, rows, no), BF16),
        pltpu.VMEM((nmu, rows, no), BF16),
        pltpu.VMEM((2, nmu, rows, no), BF16),
        pltpu.VMEM((nmu, rows, no), BF16),
        pltpu.VMEM((2, nmu, rows, no), BF16),
        pltpu.VMEM((lanes, rows * nmu, 128), F32),
        pltpu.VMEM((rows, nmu, no), BF16),
        pltpu.VMEM((2, RING, UNIT, 2 * rows, no), F32),
        pltpu.VMEM((no, no), F32),
        pltpu.VMEM((no // 2, no), F32),
        pltpu.VMEM((ncol, chunk, no), F32),
        pltpu.VMEM((ncol, chunk, no), F32),
        pltpu.VMEM((nrow // 2, chunk, no), F32),
        pltpu.VMEM((ncol, chunk, no), F32),
        pltpu.VMEM((ncol, chunk, no), F32),
        dma((NBUF,)),
        dma,
        dma,
        dma((NY - 1,)),
        dma((NY - 1,)),
        dma((NY - 1, nrow // 2 - 1)),
        dma((NY - 1, nrow // 2 - 1)),
        dma((NY - 1, nrow // 2)),
        dma((NY - 1, nrow // 2)),
        dma((2, 2, nmu // 2 // UNIT, 2)),
        dma((2, 2, nmu // 2 // UNIT, 2)),
        dma((2, 2, nmu // 2 // UNIT)),
        dma((2, 2, nmu // 2 // UNIT)),
        dma((2, 2, nmu // 2 // UNIT)),
        dma((2, 2, nmu // 2 // UNIT)),
        dma((2, nmu)),
        dma((2, nmu)),
        dma,
        dma,
        dma((ncol,)),
        dma((ncol,)),
        dma((nrow // 2,)),
        dma((nrow // 2,)),
        dma((ncol,)),
        dma((ncol,)),
        dma,
        dma,
        dma,
    ]
    anywhere = pl.BlockSpec(memory_space=pl.ANY)
    flops = 2 * rows * nmu * no * (basis + ncol * rows + no)
    return pl.pallas_call(
        functools.partial(kernel, dims),
        out_shape=(
            pltpu.VMEM((rows, nmu, no), BF16),
            pltpu.VMEM((no, no), F32),
        ),
        in_specs=[
            anywhere,
            pl.BlockSpec(memory_space=pltpu.SMEM),
            anywhere,
            anywhere,
        ],
        out_specs=(anywhere, pl.BlockSpec(memory_space=pltpu.VMEM)),
        scratch_shapes=scratch,
        compiler_params=pltpu.CompilerParams(
            collective_id=0, has_side_effects=True, vmem_limit_bytes=58 * 1024 * 1024
        ),
        cost_estimate=pl.CostEstimate(
            flops=flops, bytes_accessed=2 * rows * nmu * (basis + no), transcendentals=0
        ),
    )(integrals, occupancy.T, coeffs, metric)


def solution(mesh):
    placed = (P("col", "row", None), P(), P(), P("col", None))
    return jax.shard_map(
        functools.partial(on_device, mesh.shape["col"], mesh.shape["row"]),
        mesh=mesh,
        in_specs=placed,
        out_specs=(P("col", "row", None), P()),
        check_vma=False,
    )
```

```python
import functools

import jax
import jax.numpy as jnp
from jax import lax
from jax.experimental import pallas as pl
from jax.experimental.pallas import tpu as pltpu
from jax.sharding import PartitionSpec as P

BLK = 128
NX = 4
NY = 4
QC = 32
UNIT = 2
AHEAD = 2
LAG = 1
NBUF = 4
OPP, RIGHT, LEFT, OWN = range(4)
MESH = pl.DeviceIdType.MESH
F32 = jnp.float32
BF16 = jnp.bfloat16


def kernel(
    dims, integrals, occupancy, coeffs, metric, fitted, pair,
    ibuf, cbuf, cmask, stage_a, stage_b, mb, mbt, hbuf, opp_out, side_out, opp_in, side_in,
    rows_f32, out_bf16, pbuf, pair_acc, red0, mine, red1, red2, red3, red4,
    in_sem, c_sem, m_loc, m_send, m_recv, m2_send, m2_recv, m3_send, m3_recv,
    ag_send, ag_recv, fw_send, fw_recv, op_send, op_recv, sd_send, sd_recv,
    r0_send, r0_recv, r1_send, r1_recv, r2_send, r2_recv, r3_send, r3_recv,
    r4_send, r4_recv, out_sem,
):
    ncol, nrow, rows, nmu, basis, no, scale = dims
    half = rows // 2
    kq = NX * rows
    per_set = nmu // 2
    nset = per_set // UNIT
    nz = nrow // 2
    row = lax.axis_index("row")
    sib = row + 1 - 2 * lax.rem(row, 2)
    col = lax.axis_index("col")
    x = lax.rem(col, NX)
    y = lax.div(col, NX)
    nab = rows // BLK
    nch = rows // QC

    def col_x(d):
        return y * NX + lax.rem(x + d, NX)

    def col_y(d):
        return lax.rem(y + d, NY) * NX + x

    ag_to = ((col_x(1), col_x(NX - 1)), (col_y(1), col_y(NY - 1)))
    rs_to = (ag_to[1], ag_to[0])
    at_x = tuple(lax.rem(x + d, NX) for d in (0, NX - 1, 1, 2))
    held = (at_x, (OWN, LEFT, RIGHT, OPP))

    def in_copy(ch):
        q = pl.ds(ch * QC, QC)
        slot = lax.rem(ch, NBUF)
        return pltpu.make_async_copy(integrals.at[q], ibuf.at[slot], in_sem.at[slot])

    c_copy = pltpu.make_async_copy(coeffs, cbuf, c_sem)
    c_copy.start()

    @pl.loop(0, NBUF)
    def _(ch):
        in_copy(ch).start()

    def m_own():
        src = metric.at[:, pl.ds(pl.multiple_of(y * kq, 128), kq)]
        return pltpu.make_async_copy(src, mb.at[OWN], m_loc)

    m_own().start()

    barrier = pltpu.get_barrier_semaphore()

    @pl.loop(1, ncol)
    def _(d):
        pl.semaphore_signal(
            barrier, inc=1, device_id=(row, lax.rem(col + d, ncol)), device_id_type=MESH
        )

    @pl.loop(1, nrow)
    def _(d):
        pl.semaphore_signal(
            barrier, inc=1, device_id=(lax.rem(row + d, nrow), col), device_id_type=MESH
        )

    slot_of = {1: RIGHT, 2: OPP, 3: LEFT}
    share = rows // nrow

    def rows_of(r):
        return pl.ds(pl.multiple_of(r * share, 16), share)

    def m_copy(d):
        yd = lax.rem(y + d, NY)
        return pltpu.make_async_remote_copy(
            src_ref=metric.at[rows_of(row), pl.ds(pl.multiple_of(yd * kq, 128), kq)],
            dst_ref=mb.at[slot_of[NY - d], rows_of(row)],
            send_sem=m_send.at[d - 1],
            recv_sem=m_recv.at[NY - d - 1],
            device_id=(row, col_y(d)),
            device_id_type=MESH,
        )

    def m_landed(s):
        return pltpu.make_async_remote_copy(
            src_ref=metric.at[rows_of(row), pl.ds(0, kq)],
            dst_ref=mb.at[slot_of[s], rows_of(row)],
            send_sem=m_send.at[s - 1],
            recv_sem=m_recv.at[s - 1],
            device_id=(row, col_y(s)),
            device_id_type=MESH,
        )

    def along_z(d):
        return lax.rem(row + 2 * d, nrow)

    def m_share(s, d):
        blk = mb.at[slot_of[s], rows_of(row)]
        return pltpu.make_async_remote_copy(
            src_ref=blk,
            dst_ref=blk,
            send_sem=m2_send.at[s - 1, d - 1],
            recv_sem=m2_recv.at[s - 1, nz - d - 1],
            device_id=(along_z(d), col),
            device_id_type=MESH,
        )

    def m_shared(s, d):
        blk = mb.at[slot_of[s], rows_of(along_z(d))]
        return pltpu.make_async_remote_copy(
            src_ref=blk,
            dst_ref=blk,
            send_sem=m2_send.at[s - 1, d - 1],
            recv_sem=m2_recv.at[s - 1, d - 1],
            device_id=(along_z(d), col),
            device_id_type=MESH,
        )

    def m_pass(s, d, mine=True):
        src = along_z(d) if mine else lax.rem(sib + 2 * d, nrow)
        blk = mb.at[slot_of[s], rows_of(src)]
        return pltpu.make_async_remote_copy(
            src_ref=blk,
            dst_ref=blk,
            send_sem=m3_send.at[s - 1, d],
            recv_sem=m3_recv.at[s - 1, d],
            device_id=(sib, col),
            device_id_type=MESH,
        )

    c_copy.wait()
    def make_mask(ab):
        @pl.loop(0, basis // BLK, unroll=4)
        def _(nb):
            on = jnp.full((BLK, no), occupancy[nb, col * nab + ab], jnp.int32) > 0
            at = pl.ds(pl.multiple_of(nb * BLK, BLK), BLK)
            kept = jnp.where(on, cbuf[at, :].astype(F32), 0.0)
            cmask[ab, at, :] = kept.astype(BF16)

    make_mask(0)

    pl.semaphore_wait(barrier, ncol + nrow - 2)

    for d in (2, 1, 3):
        m_copy(d).start()

    def transform(ch, ab, to):
        rowsin = ibuf[lax.rem(ch, NBUF)].reshape(QC * nmu, basis)
        res = jnp.dot(rowsin, cmask[ab], preferred_element_type=F32)
        for h in range(no // 128):
            to[h] = res[:, h * 128 : (h + 1) * 128]

    def relayout(ch, frm):
        q0 = pl.multiple_of(ch * QC, QC)
        for mu in range(nmu):
            own = held[mu // per_set][0]
            for h in range(no // 128):
                got = frm[h, pl.ds(mu, QC, stride=nmu), :]
                hbuf[mu, own, pl.ds(q0, QC), h * 128 : (h + 1) * 128] = got.astype(BF16)

    def mus(st, k):
        return pl.ds(st * per_set + k * UNIT, UNIT)

    def ag_copy(st, side, k, hf, blk=None, to=None):
        part_rows = pl.ds(hf * half, half)
        src = held[st][0] if blk is None else blk
        dst = (at_x[0], (LEFT, RIGHT)[side])[st] if to is None else to
        return pltpu.make_async_remote_copy(
            src_ref=hbuf.at[mus(st, k), src, part_rows],
            dst_ref=hbuf.at[mus(st, k), dst, part_rows],
            send_sem=ag_send.at[st, side, k, hf],
            recv_sem=ag_recv.at[st, side, k, hf],
            device_id=(row, ag_to[st][side]),
            device_id_type=MESH,
        )

    def ag_wait(st, side, k, hf):
        blk = held[st][1 + side]
        ag_copy(st, side, k, hf, blk, blk).wait_recv()

    def fw_copy(st, side, k, blk=None, to=None):
        part_rows = pl.ds(side * half, half)
        src = held[st][1 + side] if blk is None else blk
        dst = (at_x[1 + side], OPP)[st] if to is None else to
        return pltpu.make_async_remote_copy(
            src_ref=hbuf.at[mus(st, k), src, part_rows],
            dst_ref=hbuf.at[mus(st, k), dst, part_rows],
            send_sem=fw_send.at[st, side, k],
            recv_sem=fw_recv.at[st, side, k],
            device_id=(row, ag_to[st][side]),
            device_id_type=MESH,
        )

    def fw_wait(st, side, k):
        blk = held[st][3]
        fw_copy(st, side, k, blk, blk).wait_recv()

    def op_copy(st, side, k):
        part_rows = pl.ds(side * half, half)
        return pltpu.make_async_remote_copy(
            src_ref=opp_out.at[mus(st, k), part_rows],
            dst_ref=opp_in.at[mus(st, k), part_rows],
            send_sem=op_send.at[st, side, k],
            recv_sem=op_recv.at[st, side, k],
            device_id=(row, rs_to[st][side]),
            device_id_type=MESH,
        )

    def sd_copy(st, side, mu):
        return pltpu.make_async_remote_copy(
            src_ref=side_out.at[side, mu],
            dst_ref=side_in.at[side, mu],
            send_sem=sd_send.at[side, mu],
            recv_sem=sd_recv.at[side, mu],
            device_id=(row, rs_to[st][side]),
            device_id_type=MESH,
        )

    def ag_start(st, k):
        for step in range(2):
            ag_copy(st, 0, k, step).start()
            ag_copy(st, 1, k, 1 - step).start()

    def forward(st, k):
        for side in range(2):
            ag_wait(st, side, k, side)
            fw_copy(st, side, k).start()

    def product(st, k):
        block = (mb, mbt)[st]
        for side in range(2):
            ag_wait(st, side, k, 1 - side)
            fw_wait(st, side, k)

        @pl.loop(0, UNIT)
        def _(m):
            mu = st * per_set + k * UNIT + m
            full = hbuf[mu].reshape(kq, no)
            got = jnp.dot(block[...].reshape(NY * rows, kq), full, preferred_element_type=F32)
            opp_out[mu] = got[:rows].astype(BF16)
            for side in range(2):
                at = (1 + side) * rows
                first = got[at : at + half]
                second = got[at + half : at + rows]
                plain = pl.ds((1 - side) * half, half)
                side_out[side, mu, plain] = (second, first)[side].astype(BF16)
                pbuf[st, lax.rem(k, 3), m, pl.ds(side * half, half)] = (first, second)[side]
            pbuf[st, lax.rem(k, 3), m, pl.ds(rows, rows)] = got[3 * rows :]

        op_copy(st, 0, k).start()
        op_copy(st, 1, k).start()

    def sides(k):
        for m in range(UNIT):
            for st in range(2):
                mu = st * per_set + k * UNIT + m
                for side in range(2):
                    if m == 0:
                        op_copy(st, side, k).wait_recv()
                    at = pl.ds(side * half, half)
                    side_out[side, mu, at] = (
                        pbuf[st, lax.rem(k, 3), m, at] + opp_in[mu, at].astype(F32)
                    ).astype(BF16)
                    sd_copy(st, side, mu).start()

    pair_acc[...] = jnp.zeros_like(pair_acc)

    def finish(k):
        @pl.loop(0, UNIT)
        def _(m):
            pairs = []
            for st in range(2):
                for side in range(2):
                    sd_copy(st, side, st * per_set + k * UNIT + m).wait_recv()
            for st in range(2):
                mu = st * per_set + k * UNIT + m
                own = pbuf[st, lax.rem(k, 3), m, pl.ds(rows, rows)]
                total = own + side_in[0, mu].astype(F32) + side_in[1, mu].astype(F32)
                done = total.astype(BF16)
                back = done.astype(F32)
                for h in range(no // 128):
                    at = pl.ds(mu, rows, stride=nmu)
                    rows_f32[h, at, :] = back[:, h * 128 : (h + 1) * 128]
                pairs.append(done)
            both = jnp.concatenate(pairs, axis=0)
            pair_acc[...] += lax.dot_general(
                both, both, (((0,), (0,)), ((), ())), preferred_element_type=F32
            )

    quarter = rows // 4

    def send_quarter(qt):
        part_rows = pl.ds(pl.multiple_of(qt * quarter, quarter), quarter)
        for k in range(AHEAD):
            for st in range(2):
                for side in range(2):
                    pltpu.make_async_remote_copy(
                        src_ref=hbuf.at[mus(st, k), held[st][0], part_rows],
                        dst_ref=hbuf.at[
                            mus(st, k), (at_x[0], (LEFT, RIGHT)[side])[st], part_rows
                        ],
                        send_sem=ag_send.at[st, side, k, lax.div(qt, 2)],
                        recv_sem=ag_recv.at[st, side, k, lax.div(qt, 2)],
                        device_id=(row, ag_to[st][side]),
                        device_id_type=MESH,
                    ).start()

    stage_b[...] = jnp.zeros_like(stage_b)

    @pl.loop(0, nch // 2)
    def _(j):
        ch = 2 * j
        ab = lax.div(ch * QC, BLK)

        for later in range(1, nab):

            @pl.when(ch == later * (nch // nab))
            def _():
                make_mask(later)

        in_copy(ch).wait()
        in_copy(ch + 1).wait()
        transform(ch, ab, stage_a)
        relayout(lax.max(ch - 1, 0), stage_b)

        @pl.when(j >= 1)
        def _():
            send_quarter(j - 1)

        @pl.when(j == 1)
        def _():
            for s in (2, 1, 3):
                m_landed(s).wait_recv()
                for d in (2, 1, 3):
                    m_share(s, d).start()
                m_pass(s, 0).start()

        transform(ch + 1, ab, stage_b)
        relayout(ch, stage_a)

        @pl.when(ch + NBUF < nch)
        def _():
            in_copy(ch + NBUF).start()
            in_copy(ch + NBUF + 1).start()

    relayout(nch - 1, stage_b)
    send_quarter(nch // 2 - 1)

    def metric_sent():
        for s in range(1, NY):
            m_copy(s).wait_send()
            for d in range(nz):
                m_pass(s, d).wait_send()
            for d in range(1, nz):
                m_share(s, d).wait_send()

    def sent_early(k):
        for st in range(2):
            for side in range(2):
                for hf in range(2):
                    ag_copy(st, side, k, hf).wait_send()
                fw_copy(st, side, k).wait_send()
                op_copy(st, side, k).wait_send()

    def sent_late(k):
        for st in range(2):
            for side in range(2):
                for m in range(UNIT):
                    sd_copy(st, side, st * per_set + k * UNIT + m).wait_send()

    def metric_ready():
        m_own().wait()
        for d in range(nz):
            for s in (2, 1, 3):
                m_pass(s, d, False).wait_recv()

    def transpose_metric():
        offs = {OPP: 2, RIGHT: 1, LEFT: NX - 1, OWN: 0}
        for to, d in offs.items():
            at = pl.ds(pl.multiple_of(lax.rem(x + d, NX) * rows, 128), rows)

            @pl.loop(0, NY)
            def _(s):
                mbt[to, :, pl.ds(pl.multiple_of(s * rows, 128), rows)] = mb[s, :, at].T

    @pl.loop(0, nset + LAG + 2)
    def _(k):
        @pl.when(k + AHEAD < nset)
        def _():
            ag_start(0, k + AHEAD)
            ag_start(1, k + AHEAD)

        @pl.when(k < nset)
        def _():
            forward(0, k)
            forward(1, k)

        @pl.when(k == 0)
        def _():
            for s in (2, 1, 3):
                for d in (1, 3, 2):
                    m_shared(s, d).wait_recv()
                    m_pass(s, d).start()

        @pl.when((k >= LAG) & (k < nset + LAG))
        def _():
            @pl.when(k == LAG)
            def _():
                metric_ready()

            product(0, k - LAG)

            @pl.when(k == LAG)
            def _():
                transpose_metric()

            product(1, k - LAG)

        @pl.when((k >= LAG + 1) & (k < nset + LAG + 1))
        def _():
            sides(k - LAG - 1)
            sent_early(k - LAG - 1)

        @pl.when(k == LAG + 1)
        def _():
            metric_sent()

        @pl.when(k >= LAG + 2)
        def _():
            finish(k - LAG - 2)

        @pl.when((k >= LAG + 2) & (k < nset + LAG + 1))
        def _():
            sent_late(k - LAG - 2)

    chunk = no // 2 // ncol
    core = lax.rem(row, 2)
    mid = no // 2
    mine_at = pl.ds(pl.multiple_of(core * mid, 8), mid)
    theirs_at = pl.ds(pl.multiple_of((1 - core) * mid, 8), mid)

    r0_copy = pltpu.make_async_remote_copy(
        src_ref=pair_acc.at[theirs_at],
        dst_ref=red0,
        send_sem=r0_send,
        recv_sem=r0_recv,
        device_id=(sib, col),
        device_id_type=MESH,
    )
    r0_copy.start()

    def r1_copy(d):
        to = lax.rem(col + d, ncol)
        return pltpu.make_async_remote_copy(
            src_ref=mine.at[to],
            dst_ref=red1.at[col],
            send_sem=r1_send.at[d],
            recv_sem=r1_recv.at[col],
            device_id=(row, to),
            device_id_type=MESH,
        )

    def r1_landed(src):
        return pltpu.make_async_remote_copy(
            src_ref=mine.at[src],
            dst_ref=red1.at[src],
            send_sem=r1_send.at[0],
            recv_sem=r1_recv.at[src],
            device_id=(row, src),
            device_id_type=MESH,
        )

    def r2_copy(d):
        z = lax.div(row, 2)
        return pltpu.make_async_remote_copy(
            src_ref=red2.at[z],
            dst_ref=red2.at[z],
            send_sem=r2_send.at[d],
            recv_sem=r2_recv.at[z],
            device_id=(along_z(d), col),
            device_id_type=MESH,
        )

    def r2_landed(d):
        z = lax.div(along_z(d), 2)
        return pltpu.make_async_remote_copy(
            src_ref=red2.at[z],
            dst_ref=red2.at[z],
            send_sem=r2_send.at[d],
            recv_sem=r2_recv.at[z],
            device_id=(along_z(d), col),
            device_id_type=MESH,
        )

    def r3_copy(d):
        to = lax.rem(col + d, ncol)
        return pltpu.make_async_remote_copy(
            src_ref=red3.at[col],
            dst_ref=red3.at[col],
            send_sem=r3_send.at[d],
            recv_sem=r3_recv.at[col],
            device_id=(row, to),
            device_id_type=MESH,
        )

    def r3_landed(src):
        return pltpu.make_async_remote_copy(
            src_ref=red3.at[src],
            dst_ref=red3.at[src],
            send_sem=r3_send.at[0],
            recv_sem=r3_recv.at[src],
            device_id=(row, src),
            device_id_type=MESH,
        )

    def lay_out(begin, end):
        @pl.loop(begin, end)
        def _(ch):
            at = pl.ds(pl.multiple_of(ch * QC * nmu, QC), QC * nmu)
            for h in range(no // 128):
                out_bf16[pl.ds(ch * QC, QC), :, h * 128 : (h + 1) * 128] = (
                    rows_f32[h, at, :].astype(BF16).reshape(QC, nmu, 128)
                )

    lay_out(0, nch // 4)
    r0_copy.wait_recv()
    mine[...] = (pair_acc[mine_at] + red0[...]).reshape(ncol, chunk, no)

    @pl.loop(1, ncol, unroll=ncol - 1)
    def _(d):
        r1_copy(d).start()

    red1[col] = mine[col]

    lay_out(nch // 4, nch)
    sent_late(nset - 1)

    out_copy = pltpu.make_async_copy(out_bf16, fitted, out_sem)
    out_copy.start()

    @pl.loop(1, ncol, unroll=ncol - 1)
    def _(d):
        r1_landed(lax.rem(col + d, ncol)).wait_recv()

    total = red1[0]
    for c in range(1, ncol):
        total = total + red1[c]
    red2[lax.div(row, 2)] = total
    for d in (2, 1, 3):
        r2_copy(d).start()
    for d in (1, 3, 2):
        r2_landed(d).wait_recv()

    total = red2[0]
    for z in range(1, nz):
        total = total + red2[z]
    red3[col] = total * F32(scale)

    @pl.loop(1, ncol, unroll=ncol - 1)
    def _(d):
        r3_copy(d).start()

    @pl.loop(1, ncol, unroll=ncol - 1)
    def _(d):
        r3_landed(lax.rem(col + d, ncol)).wait_recv()

    r4_copy = pltpu.make_async_remote_copy(
        src_ref=red3,
        dst_ref=red4,
        send_sem=r4_send,
        recv_sem=r4_recv,
        device_id=(sib, col),
        device_id_type=MESH,
    )
    r4_copy.start()
    pair[mine_at] = red3[...].reshape(mid, no)

    r0_copy.wait_send()

    @pl.loop(1, ncol)
    def _(d):
        r1_copy(d).wait_send()
        r3_copy(d).wait_send()

    for d in range(1, nz):
        r2_copy(d).wait_send()

    r4_copy.wait_recv()
    pair[theirs_at] = red4[...].reshape(mid, no)
    r4_copy.wait_send()
    out_copy.wait()


def on_device(ncol, nrow, integrals, occupancy, coeffs, metric):
    rows, nmu, basis = integrals.shape
    no = coeffs.shape[1]
    kq = NX * rows
    chunk = no // 2 // ncol
    scale = 1.0 / (rows * ncol * nmu * nrow)
    dims = (ncol, nrow, rows, nmu, basis, no, scale)
    lanes = no // 128
    dma = pltpu.SemaphoreType.DMA
    scratch = [
        pltpu.VMEM((NBUF, QC, nmu, basis), BF16),
        pltpu.VMEM((basis, no), BF16),
        pltpu.VMEM((rows // BLK, basis, no), BF16),
        pltpu.VMEM((lanes, QC * nmu, 128), F32),
        pltpu.VMEM((lanes, QC * nmu, 128), F32),
        pltpu.VMEM((NY, rows, kq), BF16),
        pltpu.VMEM((NX, rows, kq), BF16),
        pltpu.VMEM((nmu, NX, rows, no), BF16),
        pltpu.VMEM((nmu, rows, no), BF16),
        pltpu.VMEM((2, nmu, rows, no), BF16),
        pltpu.VMEM((nmu, rows, no), BF16),
        pltpu.VMEM((2, nmu, rows, no), BF16),
        pltpu.VMEM((lanes, rows * nmu, 128), F32),
        pltpu.VMEM((rows, nmu, no), BF16),
        pltpu.VMEM((2, 3, UNIT, 2 * rows, no), F32),
        pltpu.VMEM((no, no), F32),
        pltpu.VMEM((no // 2, no), F32),
        pltpu.VMEM((ncol, chunk, no), F32),
        pltpu.VMEM((ncol, chunk, no), F32),
        pltpu.VMEM((nrow // 2, chunk, no), F32),
        pltpu.VMEM((ncol, chunk, no), F32),
        pltpu.VMEM((ncol, chunk, no), F32),
        dma((NBUF,)),
        dma,
        dma,
        dma((NY - 1,)),
        dma((NY - 1,)),
        dma((NY - 1, nrow // 2 - 1)),
        dma((NY - 1, nrow // 2 - 1)),
        dma((NY - 1, nrow // 2)),
        dma((NY - 1, nrow // 2)),
        dma((2, 2, nmu // 2 // UNIT, 2)),
        dma((2, 2, nmu // 2 // UNIT, 2)),
        dma((2, 2, nmu // 2 // UNIT)),
        dma((2, 2, nmu // 2 // UNIT)),
        dma((2, 2, nmu // 2 // UNIT)),
        dma((2, 2, nmu // 2 // UNIT)),
        dma((2, nmu)),
        dma((2, nmu)),
        dma,
        dma,
        dma((ncol,)),
        dma((ncol,)),
        dma((nrow // 2,)),
        dma((nrow // 2,)),
        dma((ncol,)),
        dma((ncol,)),
        dma,
        dma,
        dma,
    ]
    anywhere = pl.BlockSpec(memory_space=pl.ANY)
    flops = 2 * rows * nmu * no * (basis + ncol * rows + no)
    return pl.pallas_call(
        functools.partial(kernel, dims),
        out_shape=(
            pltpu.VMEM((rows, nmu, no), BF16),
            pltpu.VMEM((no, no), F32),
        ),
        in_specs=[
            anywhere,
            pl.BlockSpec(memory_space=pltpu.SMEM),
            anywhere,
            anywhere,
        ],
        out_specs=(anywhere, pl.BlockSpec(memory_space=pltpu.VMEM)),
        scratch_shapes=scratch,
        compiler_params=pltpu.CompilerParams(
            collective_id=0, has_side_effects=True, vmem_limit_bytes=58 * 1024 * 1024
        ),
        cost_estimate=pl.CostEstimate(
            flops=flops, bytes_accessed=2 * rows * nmu * (basis + no), transcendentals=0
        ),
    )(integrals, occupancy.T, coeffs, metric)


def solution(mesh):
    placed = (P("col", "row", None), P(), P(), P("col", None))
    return jax.shard_map(
        functools.partial(on_device, mesh.shape["col"], mesh.shape["row"]),
        mesh=mesh,
        in_specs=placed,
        out_specs=(P("col", "row", None), P()),
        check_vma=False,
    )
```
